32 devices in a mesh: feature: 4 (over y, x), kvhead: 2 (over core), seq: 4 (over z).
Axes of the slice: x: 2, y: 2, z: 4, core: 2. Of those that a mesh axis runs over, the one named last changes fastest.
Arguments:
- queries: float32 [1024, 40, 128], P('seq', 'kvhead'), may hold values from -6 to 6
- keys: float32 [1024, 8, 128], P('seq', 'kvhead'), may hold values from -6 to 6
- values: float32 [1024, 8, 128], P('seq', 'kvhead'), may hold values from -6 to 6
- w_out: float32 [5120, 5120], P('kvhead', ('feature', 'seq')), may hold values from -0.078125 to 0.078125
Outputs:
- projected: float32 [1024, 5120], P(('seq', 'feature'), 'kvhead')
The draws below stay inside these ranges and needn't reach their ends.
All inputs are finite; a program needn't handle non-finite values.
Results may differ from the reference program's by a relative error of at most 0.0003.
Values sent between devices are 32-bit elements; how exact they have to be, the bound alone decides.
No kernel may reach another device: no remote copies, remote signals or barrier semaphores. Data moves between devices by JAX's collectives and lax.ppermute only.
A program may use at most 192 MiB of HBM per device.

```python
import jax
import jax.numpy as jnp
from jax import lax

D = 5120
QH = 40
KVH = 8
HD = 128
TOKENS = 1024


def block_levels(rng, shape, cuts, smallest, top_value):
    factor_of, own = 1.0, jax.random.fold_in(rng, 6)
    for dim, parts in cuts:
        heights = jnp.exp(jax.random.uniform(jax.random.fold_in(own, dim), (parts,), jnp.float32, smallest / len(cuts), top_value / len(cuts)))
        factor_of = factor_of * jnp.repeat(heights, shape[dim] // parts).reshape([-1 if axis == dim else 1 for axis in range(len(shape))])
    return factor_of


def gaussian(key, extent, deviation, limit, pieces=(), kind=jnp.bfloat16):
    entries = jax.random.normal(key, extent, jnp.float32) * deviation
    if len(pieces) > 0:
        entries = block_levels(key, extent, pieces, -0.22, 0.18) * entries
    return jnp.clip(entries, min=-limit, max=limit).astype(kind)


def setup_inputs(seed: int = 0) -> dict:
    streams_of = jax.random.split(jax.random.key(seed), 5)
    queries = gaussian(streams_of[0], (TOKENS, QH, HD), 1.0, 6.0, ((0, 4), (1, 2)), jnp.float32)
    keys = gaussian(streams_of[1], (TOKENS, KVH, HD), 1.0, 6.0, ((0, 4), (1, 2)), jnp.float32)
    values = gaussian(streams_of[2], (TOKENS, KVH, HD), 1.0, 6.0, ((0, 4), (1, 2)), jnp.float32)
    w_out = gaussian(streams_of[3], (QH * HD, D), (QH * HD) ** -0.5, 0.078125, ((0, 2), (1, 16)), jnp.float32)
    return dict(queries=queries, keys=keys, values=values, w_out=w_out)


def reference(queries, keys, values, w_out):
    block = 512 if TOKENS % 512 == 0 else TOKENS
    count = TOKENS // block
    group = QH // KVH
    scaled = (queries * (HD ** -0.5)).reshape(count, block, KVH, group, HD)
    key_blocks = keys.reshape(count, block, KVH, HD)
    value_blocks = values.reshape(count, block, KVH, HD)
    offsets = jnp.arange(block, dtype=jnp.int32)

    def one_block(index):
        query_part = lax.dynamic_index_in_dim(scaled, index, 0, keepdims=False)

        def key_step(other, carry):
            numerator, denominator = carry
            key_part = lax.dynamic_index_in_dim(key_blocks, other, 0, keepdims=False)
            value_part = lax.dynamic_index_in_dim(value_blocks, other, 0, keepdims=False)
            scores = jnp.einsum("tkgd,skd->tkgs", query_part, key_part, precision=lax.Precision.HIGHEST)
            squared = scores * scores
            query_pos = index * block + offsets
            key_pos = other * block + offsets
            allowed = key_pos[None, :] <= query_pos[:, None]
            squared = jnp.where(allowed[:, None, None, :], squared, jnp.float32(0.0))
            numerator = numerator + jnp.einsum("tkgs,skd->tkgd", squared, value_part, precision=lax.Precision.HIGHEST)
            denominator = denominator + jnp.sum(squared, axis=-1)
            return numerator, denominator

        start = (jnp.zeros((block, KVH, group, HD), jnp.float32), jnp.zeros((block, KVH, group), jnp.float32))
        numerator, denominator = lax.fori_loop(0, index + 1, key_step, start)
        attended = numerator / (denominator[..., None] + 1.0)
        return attended.reshape(block, QH * HD)

    attended = lax.map(one_block, jnp.arange(count, dtype=jnp.int32)).reshape(TOKENS, QH * HD)
    return jnp.dot(attended, w_out, precision=lax.Precision.HIGHEST, preferred_element_type=jnp.float32)
```

```python
import functools

import jax
import jax.numpy as jnp
from jax import lax
from jax.experimental import pallas as pl
from jax.experimental.pallas import tpu as pltpu
from jax.sharding import PartitionSpec as P

F32 = jnp.float32
BF16 = jnp.bfloat16
VMEM_LIMIT = 48 * 1024 * 1024
NT = (((1,), (1,)), ((), ()))


def split(a):
    high = a.astype(BF16)
    return high, (a - high.astype(F32)).astype(BF16)


def mm(a, b):
    return jnp.dot(a, b, preferred_element_type=F32)


def params():
    return pltpu.CompilerParams(vmem_limit_bytes=VMEM_LIMIT)


def smem():
    return pl.BlockSpec(memory_space=pltpu.SMEM)


def vmem(n):
    return [pl.BlockSpec(memory_space=pltpu.VMEM)] * n


def ring_at(place, n):
    half = (n + 1) // 2
    return jnp.where(place < half, 2 * place, 2 * (n - place) - 1)


def ring_place(index, n):
    return jnp.where(index % 2 == 0, index // 2, n - 1 - index // 2)


def ring_perm(n, step):
    order = list(range(0, n, 2)) + list(range(1, n, 2))[::-1]
    return [(order[i], order[(i + step) % n]) for i in range(n)]


def prepare_keys(pairs):
    n = len(pairs)
    _, rows, d = pairs[0].shape

    def kernel(*refs):
        kt, vv = refs[n:]
        for j in range(n):
            at = pl.ds(j * rows, rows)
            k_high, k_low = split(refs[j][0].T)
            kt[0:d, at] = k_high
            kt[d : 2 * d, at] = k_high
            kt[2 * d : 3 * d, at] = k_low
            v_high, v_low = split(refs[j][1])
            vv[at, 0:d] = v_high
            vv[at, d : 2 * d] = v_low
            below = pl.ds((n + j) * rows, rows)
            vv[below, 0:d] = v_high
            vv[below, d : 2 * d] = jnp.zeros((rows, d), BF16)

    return pl.pallas_call(
        kernel,
        out_shape=(
            jax.ShapeDtypeStruct((3 * d, n * rows), BF16),
            jax.ShapeDtypeStruct((2 * n * rows, 2 * d), BF16),
        ),
        in_specs=vmem(n),
        out_specs=tuple(vmem(2)),
        compiler_params=params(),
        cost_estimate=pl.CostEstimate(flops=0, bytes_accessed=6 * n * rows * d * 4, transcendentals=0),
        name="prepare_keys",
    )(*pairs)


def attend(meta, blocks, slots, kt, vv):
    group, rows, d = blocks[0].shape
    count = kt.shape[1] // rows
    n = len(blocks)
    scale = d ** (-0.5)

    def kernel(meta_ref, *refs):
        kt_ref, vv_ref, out = refs[n:]
        key_row = lax.broadcasted_iota(jnp.int32, (1, rows), 1)
        key_at = jnp.concatenate([key_row + meta_ref[j] * rows for j in range(count)], axis=1)
        row = lax.broadcasted_iota(jnp.int32, (rows, 1), 0)
        for i in range(n):
            allowed = key_at <= row + meta_ref[slots[i]] * rows

            def one(h, carry):
                q_high, q_low = split(refs[i][h] * scale)
                scores = mm(jnp.concatenate([q_high, q_low, q_high], axis=1), kt_ref[...])
                squared = jnp.where(allowed, scores * scores, 0.0)
                total = jnp.sum(squared, axis=1, keepdims=True)
                s_high, s_low = split(squared)
                both = mm(jnp.concatenate([s_high, s_low], axis=1), vv_ref[...])
                numerator = both[:, 0:d] + both[:, d : 2 * d]
                at = pl.ds(pl.multiple_of(h * d, d), d)
                out[pl.ds(i * rows, rows), at] = numerator / (total + 1.0)
                return carry

            lax.fori_loop(0, group, one, 0)

    return pl.pallas_call(
        kernel,
        out_shape=jax.ShapeDtypeStruct((n * rows, group * d), F32),
        in_specs=[smem()] + vmem(n + 2),
        out_specs=vmem(1)[0],
        compiler_params=params(),
        cost_estimate=pl.CostEstimate(
            flops=2 * n * group * rows * count * rows * d * 10,
            bytes_accessed=n * group * rows * d * 8 + kt.size * 2 + vv.size * 2,
            transcendentals=0,
        ),
        name="attend",
    )(meta, *blocks, kt, vv)


def prepare_weights(meta, pieces):
    n = len(pieces)
    columns, k = pieces[0].shape

    def kernel(meta_ref, *refs):
        high, low = refs[n:]
        for i in range(n):
            group, block = meta_ref[2 * i], meta_ref[2 * i + 1]
            at = pl.ds(pl.multiple_of(block * columns, 16), columns)
            w_high, w_low = split(refs[i][...])
            high[group, at] = w_high
            low[group, at] = w_low

    shape = jax.ShapeDtypeStruct((2, n // 2 * columns, k), BF16)
    return pl.pallas_call(
        kernel,
        out_shape=(shape, shape),
        in_specs=[smem()] + vmem(n),
        out_specs=tuple(vmem(2)),
        compiler_params=params(),
        cost_estimate=pl.CostEstimate(flops=0, bytes_accessed=n * columns * k * 8, transcendentals=0),
        name="prepare_weights",
    )(meta, *pieces)


def project(meta, own, other, high, low, parts, blocks):
    rows = own.shape[0] // blocks
    columns = high.shape[1]
    cut = rows // parts

    def kernel(meta_ref, own_ref, other_ref, high_ref, low_ref, *rest):
        outs, total = rest[:parts], rest[parts]
        core, place = meta_ref[0], meta_ref[1]
        acc = None
        for ref, group in ((own_ref, core), (other_ref, 1 - core)):
            a_high, a_low = split(ref[...])
            w_high, w_low = high_ref[group], low_ref[group]
            dot = functools.partial(lax.dot_general, dimension_numbers=NT, preferred_element_type=F32)
            term = dot(a_high, w_high) + dot(a_low, w_high) + dot(a_high, w_low)
            acc = term if acc is None else acc + term
        total[...] = acc
        for e in range(parts):
            for b in range(blocks):
                start = pl.multiple_of(b * rows + (place ^ e) * cut, 8)
                outs[e][b] = total[pl.ds(start, cut)]

    shape = jax.ShapeDtypeStruct((blocks, cut, columns), F32)
    return pl.pallas_call(
        kernel,
        out_shape=(shape,) * parts,
        in_specs=[smem()] + vmem(4),
        out_specs=tuple(vmem(parts)),
        scratch_shapes=[pltpu.VMEM((blocks * rows, columns), F32)],
        compiler_params=params(),
        cost_estimate=pl.CostEstimate(
            flops=2 * blocks * rows * columns * own.shape[1] * 6,
            bytes_accessed=high.size * 4 + own.size * 8 + blocks * rows * columns * 4,
            transcendentals=0,
        ),
        name="project",
    )(meta, own, other, high, low)


def assemble(meta, parts, halves):
    n = len(parts)
    rows, columns = parts[0].shape
    width = columns // halves

    def kernel(meta_ref, *refs):
        out, held = refs[n:]
        for j in range(n):
            held[meta_ref[j]] = refs[j][...]
        pieces = [
            held[z][:, h * width : (h + 1) * width] for h in range(halves) for z in range(n)
        ]
        out[...] = jnp.concatenate(pieces, axis=1)

    return pl.pallas_call(
        kernel,
        out_shape=jax.ShapeDtypeStruct((rows, n * columns), F32),
        in_specs=[smem()] + vmem(n),
        out_specs=vmem(1)[0],
        scratch_shapes=[pltpu.VMEM((n, rows, columns), F32)],
        compiler_params=params(),
        cost_estimate=pl.CostEstimate(flops=0, bytes_accessed=8 * n * rows * columns, transcendentals=0),
        name="assemble",
    )(meta, *parts)


def by_heads(queries, keys, values, w_out):
    rows, local_heads, d = queries.shape
    kv_local = keys.shape[1]
    group = local_heads // kv_local
    parts, planes = lax.axis_size("feature"), lax.axis_size("seq")
    f, c, s = (lax.axis_index(a) for a in ("feature", "kvhead", "seq"))
    at = ring_place(s, planes)
    ints = lambda *xs: jnp.stack([jnp.asarray(x, jnp.int32) for x in xs])
    held = [ring_at((at - j) % planes, planes) for j in range(planes)]
    sender = [ring_at((at + j) % planes, planes) for j in range(planes)]

    kv = jnp.stack(
        [lax.dynamic_index_in_dim(a, f, 1, False) for a in (keys, values)]
    )
    q = lax.dynamic_slice_in_dim(queries, f * group, group, 1).transpose(1, 0, 2)
    pairs, blocks = [kv], [q]
    for _ in range(planes - 1):
        pairs.append(lax.ppermute(pairs[-1], "seq", ring_perm(planes, 1)))
        blocks.append(lax.ppermute(blocks[-1], "seq", ring_perm(planes, 1)))

    k_rows = group * d
    pieces, places = [], []
    half = parts // 2
    b = f % half
    for k in range(parts):
        k1, k0 = k // 2, k % 2
        target = half * (b ^ k1) + (c ^ k0)
        piece = lax.dynamic_slice_in_dim(w_out, target * k_rows, k_rows, 0).T
        perm = []
        for fs in range(parts):
            for cs in range(2):
                perm.append((fs * 2 + cs, (half * ((fs % half) ^ k1) + (cs ^ k0)) * 2 + fs // half))
        pieces.append(lax.ppermute(piece, ("feature", "kvhead"), perm))
        places += [(f % 2) ^ k0, (f // half) ^ k1]
    high, low = prepare_weights(ints(*places), pieces)

    kt, vv = prepare_keys(pairs)
    meta = ints(*held)
    swap = [(0, 1), (1, 0)]
    results = [None] * planes
    for slots in ((0, 1), (2,), (3,)):
        own = attend(meta, [blocks[j] for j in slots], slots, kt, vv)
        other = lax.ppermute(own, "kvhead", swap)
        out = project(ints(c, f), own, other, high, low, parts, len(slots))
        total = out[0]
        for e in range(1, parts):
            total = total + lax.ppermute(out[e], "feature", [(i, i ^ e) for i in range(parts)])
        for i, j in enumerate(slots):
            piece = total[i]
            if j:
                piece = lax.ppermute(piece, "seq", ring_perm(planes, -j))
            results[j] = piece
    return assemble(ints(*sender), results, half)


def plain(queries, keys, values, w_out):
    highest = lax.Precision.HIGHEST
    rows, local_heads, d = queries.shape
    kv_local = keys.shape[1]
    parts, planes = lax.axis_size("feature"), lax.axis_size("seq")
    f, c, s = (lax.axis_index(a) for a in ("feature", "kvhead", "seq"))
    cut = rows // parts
    q = lax.dynamic_slice_in_dim(queries, f * cut, cut, 0) * d ** (-0.5)
    q = q.reshape(cut, kv_local, local_heads // kv_local, d)
    k = lax.all_gather(keys, "seq", axis=0, tiled=True)
    v = lax.all_gather(values, "seq", axis=0, tiled=True)
    scores = jnp.einsum("tkgd,skd->kgts", q, k, precision=highest)
    row = s * rows + f * cut + jnp.arange(cut)
    allowed = jnp.arange(k.shape[0])[None, :] <= row[:, None]
    squared = jnp.where(allowed, scores * scores, 0.0)
    numerator = jnp.einsum("kgts,skd->tkgd", squared, v, precision=highest)
    denominator = jnp.transpose(jnp.sum(squared, axis=-1), (2, 0, 1))
    attended = (numerator / (denominator[..., None] + 1.0)).reshape(cut, local_heads * d)
    attended = lax.all_gather(attended, ("seq", "feature"), axis=0, tiled=True)
    partial = jnp.dot(attended, w_out, precision=highest, preferred_element_type=F32)
    whole = lax.psum(partial, "kvhead")
    mine = lax.all_to_all(whole, ("seq", "feature"), 0, 1, tiled=True)
    columns = w_out.shape[1]
    mine = mine.reshape(cut, planes, parts, columns).transpose(0, 2, 1, 3).reshape(cut, -1)
    width = mine.shape[1] // lax.axis_size("kvhead")
    return lax.dynamic_slice_in_dim(mine, c * width, width, 1)


def solution(mesh):
    in_specs = (
        P("seq", "kvhead", None),
        P("seq", "kvhead", None),
        P("seq", "kvhead", None),
        P("kvhead", ("feature", "seq")),
    )
    out_specs = P(("seq", "feature"), "kvhead")

    def local(queries, keys, values, w_out):
        parts, groups = mesh.shape["feature"], mesh.shape["kvhead"]
        body = by_heads if (groups, parts, keys.shape[1]) == (2, 4, parts) else plain
        return body(queries, keys, values, w_out)

    return jax.shard_map(local, mesh=mesh, in_specs=in_specs, out_specs=out_specs, check_vma=False)
```

```python
import functools

import jax
import jax.numpy as jnp
from jax import lax
from jax.experimental import pallas as pl
from jax.experimental.pallas import tpu as pltpu
from jax.sharding import PartitionSpec as P

F32 = jnp.float32
BF16 = jnp.bfloat16
VMEM_LIMIT = 20 * 1024 * 1024
NT = (((1,), (1,)), ((), ()))


def split(a):
    high = a.astype(BF16)
    return high, (a - high.astype(F32)).astype(BF16)


def mm(a, b):
    return jnp.dot(a, b, preferred_element_type=F32)


def after(*arrays):
    return lax.optimization_barrier(arrays)


def brief(micros=0):
    return pl.CostEstimate(flops=1 + micros * 10**9, bytes_accessed=1, transcendentals=0)


def params():
    return pltpu.CompilerParams(vmem_limit_bytes=VMEM_LIMIT)


def smem():
    return pl.BlockSpec(memory_space=pltpu.SMEM)


def vmem(n):
    return [pl.BlockSpec(memory_space=pltpu.VMEM)] * n


def ring_at(place, n):
    half = (n + 1) // 2
    return jnp.where(place < half, 2 * place, 2 * (n - place) - 1)


def ring_place(index, n):
    return jnp.where(index % 2 == 0, index // 2, n - 1 - index // 2)


def ring_perm(n, step):
    order = list(range(0, n, 2)) + list(range(1, n, 2))[::-1]
    return [(order[i], order[(i + step) % n]) for i in range(n)]


def prepare_keys(pairs):
    n = len(pairs)
    _, rows, d = pairs[0].shape

    def kernel(*refs):
        kt, vv, held, sems = refs[n:]
        copies = [pltpu.make_async_copy(refs[j], held.at[j], sems.at[j]) for j in range(n)]
        for copy in copies:
            copy.start()
        for j in range(n):
            copies[j].wait()
            at = pl.ds(j * rows, rows)
            k_high, k_low = split(held[j, 0].T)
            kt[0:d, at] = k_high
            kt[d : 2 * d, at] = k_high
            kt[2 * d : 3 * d, at] = k_low
            v_high, v_low = split(held[j, 1])
            upper, lower = pl.ds(2 * j * rows, rows), pl.ds((2 * j + 1) * rows, rows)
            vv[upper, 0:d] = v_high
            vv[upper, d : 2 * d] = v_low
            vv[lower, 0:d] = v_high
            vv[lower, d : 2 * d] = jnp.zeros((rows, d), BF16)

    return pl.pallas_call(
        kernel,
        out_shape=(
            jax.ShapeDtypeStruct((3 * d, n * rows), BF16),
            jax.ShapeDtypeStruct((2 * n * rows, 2 * d), BF16),
        ),
        in_specs=[pl.BlockSpec(memory_space=pltpu.MemorySpace.HBM)] * n,
        out_specs=tuple(vmem(2)),
        scratch_shapes=[pltpu.VMEM((n, 2, rows, d), F32), pltpu.SemaphoreType.DMA((n,))],
        compiler_params=params(),
        cost_estimate=brief(0),
        name="prepare_keys",
    )(*pairs)


def attend(meta, blocks, slots, kt, vv):
    group, rows, d = blocks[0].shape
    count = kt.shape[1] // rows
    n = len(blocks)
    scale = d ** (-0.5)

    def kernel(meta_ref, *refs):
        kt_ref, vv_ref, out, parts, acc, den = refs[n:]
        shape = (rows, rows)
        keep = lax.broadcasted_iota(jnp.int32, shape, 1) <= lax.broadcasted_iota(jnp.int32, shape, 0)

        def chunk(j, own):
            for h in range(group):
                at = pl.ds(h * rows, rows)
                scores = mm(parts[at], kt_ref[:, pl.ds(j * rows, rows)])
                squared = scores * scores
                if own:
                    squared = jnp.where(keep, squared, 0.0)
                high, low = split(squared)
                both = mm(jnp.concatenate([high, low], axis=1), vv_ref[pl.ds(2 * j * rows, 2 * rows)])
                total = jnp.broadcast_to(jnp.sum(squared, axis=1, keepdims=True), (rows, d))
                if own:
                    acc[at], den[at] = both, total
                else:
                    acc[at] += both
                    den[at] += total

        for i, slot in enumerate(slots):
            high, low = split(refs[i][...].reshape(group * rows, d) * scale)
            parts[:, 0:d] = high
            parts[:, d : 2 * d] = low
            parts[:, 2 * d : 3 * d] = high
            chunk(slot, True)
            for j in range(count):
                if j != slot:
                    pl.when(meta_ref[j] < meta_ref[slot])(functools.partial(chunk, j, False))
            for h in range(group):
                at = pl.ds(h * rows, rows)
                numerator = acc[at, 0:d] + acc[at, d : 2 * d]
                out[pl.ds(i * rows, rows), h * d : (h + 1) * d] = numerator / (den[at] + 1.0)

    return pl.pallas_call(
        kernel,
        out_shape=jax.ShapeDtypeStruct((n * rows, group * d), F32),
        in_specs=[smem()] + vmem(n + 2),
        out_specs=vmem(1)[0],
        scratch_shapes=[
            pltpu.VMEM((group * rows, 3 * d), BF16),
            pltpu.VMEM((group * rows, 2 * d), F32),
            pltpu.VMEM((group * rows, d), F32),
        ],
        compiler_params=params(),
        cost_estimate=brief(),
        name="attend",
    )(meta, *blocks, kt, vv)


def prepare_weights(meta, pieces):
    n = len(pieces)
    columns, k = pieces[0].shape

    def kernel(meta_ref, *refs):
        high, low = refs[n:]
        for i in range(n):
            at = pl.ds(pl.multiple_of(meta_ref[2 * i + 1] * columns, 16), columns)
            w_high, w_low = split(refs[i][...])
            high[meta_ref[2 * i], at] = w_high
            low[meta_ref[2 * i], at] = w_low

    shape = jax.ShapeDtypeStruct((2, n // 2 * columns, k), BF16)
    return pl.pallas_call(
        kernel,
        out_shape=(shape, shape),
        in_specs=[smem()] + vmem(n),
        out_specs=tuple(vmem(2)),
        compiler_params=params(),
        cost_estimate=brief(),
        name="prepare_weights",
    )(meta, *pieces)


def project(blocks, high, low):
    n = len(blocks)
    rows = blocks[0].shape[0]
    columns = high.shape[1]

    def kernel(*refs):
        high_ref, low_ref = refs[n : n + 2]
        a_high, a_low = split(jnp.concatenate([ref[...] for ref in refs[:n]], axis=0))
        dot = functools.partial(lax.dot_general, dimension_numbers=NT, preferred_element_type=F32)
        for half, out in ((1, refs[-1]), (0, refs[-2])):
            w_high, w_low = high_ref[half], low_ref[half]
            out[...] = dot(a_high, w_high) + dot(a_low, w_high) + dot(a_high, w_low)

    shape = jax.ShapeDtypeStruct((n * rows, columns), F32)
    return pl.pallas_call(
        kernel,
        out_shape=(shape, shape),
        in_specs=vmem(n + 2),
        out_specs=tuple(vmem(2)),
        compiler_params=params(),
        cost_estimate=brief(),
        name="project",
    )(*blocks, high, low)


def fold(meta, kept, got, blocks, order):
    rows = kept.shape[0] // blocks
    cut = rows // sum(len(group) for group in order)
    columns = kept.shape[1]

    def kernel(meta_ref, kept_ref, got_ref, *outs):
        for out, group in zip(outs, order):
            for i, e in enumerate(group):
                for b in range(blocks):
                    at = pl.ds(pl.multiple_of(b * rows + (meta_ref[0] ^ e) * cut, 8), cut)
                    out[i, b] = kept_ref[at] + got_ref[at]

    return pl.pallas_call(
        kernel,
        out_shape=tuple(
            jax.ShapeDtypeStruct((len(group), blocks, cut, columns), F32) for group in order
        ),
        in_specs=[smem()] + vmem(2),
        out_specs=tuple(vmem(len(order))),
        compiler_params=params(),
        cost_estimate=brief(),
        name="fold",
    )(meta, kept, got)


def assemble(meta, parts, halves):
    n = len(parts)
    rows, columns = parts[0].shape
    width = columns // halves

    def kernel(meta_ref, *refs):
        out, held = refs[n:]
        for j in range(n):
            held[meta_ref[j]] = refs[j][...]
        pieces = [
            held[z][:, h * width : (h + 1) * width] for h in range(halves) for z in range(n)
        ]
        out[...] = jnp.concatenate(pieces, axis=1)

    return pl.pallas_call(
        kernel,
        out_shape=jax.ShapeDtypeStruct((rows, n * columns), F32),
        in_specs=[smem()] + vmem(n),
        out_specs=vmem(1)[0],
        scratch_shapes=[pltpu.VMEM((n, rows, columns), F32)],
        compiler_params=params(),
        cost_estimate=brief(),
        name="assemble",
    )(meta, *parts)


def by_heads(queries, keys, values, w_out):
    rows, local_heads, d = queries.shape
    kv_local = keys.shape[1]
    group = local_heads // kv_local
    parts, planes = lax.axis_size("feature"), lax.axis_size("seq")
    f, c, s = (lax.axis_index(a) for a in ("feature", "kvhead", "seq"))
    at = ring_place(s, planes)
    ints = lambda *xs: jnp.stack([jnp.asarray(x, jnp.int32) for x in xs])
    held = [ring_at((at - j) % planes, planes) for j in range(planes)]
    sender = [ring_at((at + j) % planes, planes) for j in range(planes)]

    ring = lambda x, step: lax.ppermute(x, "seq", ring_perm(planes, step))
    swap = lambda x: lax.ppermute(x, "kvhead", [(0, 1), (1, 0)])

    kv = jnp.stack([lax.dynamic_index_in_dim(a, f, 1, False) for a in (keys, values)])
    pairs = [ring(kv, j) if j else kv for j in range(planes)]

    k_rows = group * d
    half = parts // 2
    turn = lambda x: lax.dynamic_slice_in_dim(w_out, x * k_rows, k_rows, 0).T
    cross = lambda x, e: lax.ppermute(x, "feature", [(i, i ^ e) for i in range(parts)])
    pieces = [cross(turn(f ^ e), e) for e in range(1, parts)]
    places = []
    for e in range(parts):
        places += [jnp.where((f ^ e) // half == c, 0, 1), (f ^ e) % half]

    q = lax.dynamic_slice_in_dim(queries, f * group, group, 1).transpose(1, 0, 2)
    *pairs, sent = after(*pairs, q)
    sent = ring(sent, 1)
    kt, vv = prepare_keys(pairs)
    meta = ints(*held)
    owns = {0: attend(meta, [q], (0,), kt, vv)}
    sent, back, *pieces = after(sent, owns[0], *pieces)
    owns[planes - 1] = ring(back, -1)
    owns[1] = attend(meta, [sent], (1,), kt, vv)
    owns[1], mine = after(owns[1], f)
    owns[2] = ring(owns[1], 1)
    high, low = prepare_weights(ints(*places), [turn(mine)] + pieces)

    results = [None] * planes
    place = ints(f)
    last, crossed = None, None
    for slots, way in (((0, 1), 1), ((3,), 2), ((2,), 0)):
        blocks = [owns[j] for j in slots]
        if last is not None:
            *blocks, _ = after(*blocks, last)
        kept, given = project(blocks, high, low)
        if slots[0] == 0:
            given, owns[planes - 1] = after(given, owns[planes - 1])
        got = swap(given)
        if way:
            keep, send = fold(place, kept, got, len(slots), ((0, 3 - way), (way, 3)))
            last, send = after(keep, send)
            both = last + cross(send, way)
            crossed = both if crossed is None else crossed
            total = both[0] + cross(both[1], 3 - way)
        else:
            got, _ = after(got, crossed)
            outs = fold(place, kept, got, len(slots), tuple((e,) for e in range(parts)))
            total = outs[0]
            for e in range(1, parts):
                total = total + cross(outs[e], e)
            total = total[0]
        for i, j in enumerate(slots):
            results[j] = ring(total[i], -j) if j else total[i]
    return assemble(ints(*sender), [results[j] for j in range(planes)], half)


def plain(queries, keys, values, w_out):
    highest = lax.Precision.HIGHEST
    rows, local_heads, d = queries.shape
    kv_local = keys.shape[1]
    parts, planes = lax.axis_size("feature"), lax.axis_size("seq")
    f, c, s = (lax.axis_index(a) for a in ("feature", "kvhead", "seq"))
    cut = rows // parts
    q = lax.dynamic_slice_in_dim(queries, f * cut, cut, 0) * d ** (-0.5)
    q = q.reshape(cut, kv_local, local_heads // kv_local, d)
    k = lax.all_gather(keys, "seq", axis=0, tiled=True)
    v = lax.all_gather(values, "seq", axis=0, tiled=True)
    scores = jnp.einsum("tkgd,skd->kgts", q, k, precision=highest)
    row = s * rows + f * cut + jnp.arange(cut)
    allowed = jnp.arange(k.shape[0])[None, :] <= row[:, None]
    squared = jnp.where(allowed, scores * scores, 0.0)
    numerator = jnp.einsum("kgts,skd->tkgd", squared, v, precision=highest)
    denominator = jnp.transpose(jnp.sum(squared, axis=-1), (2, 0, 1))
    attended = (numerator / (denominator[..., None] + 1.0)).reshape(cut, local_heads * d)
    attended = lax.all_gather(attended, ("seq", "feature"), axis=0, tiled=True)
    partial = jnp.dot(attended, w_out, precision=highest, preferred_element_type=F32)
    whole = lax.psum(partial, "kvhead")
    mine = lax.all_to_all(whole, ("seq", "feature"), 0, 1, tiled=True)
    columns = w_out.shape[1]
    mine = mine.reshape(cut, planes, parts, columns).transpose(0, 2, 1, 3).reshape(cut, -1)
    width = mine.shape[1] // lax.axis_size("kvhead")
    return lax.dynamic_slice_in_dim(mine, c * width, width, 1)


def solution(mesh):
    in_specs = (
        P("seq", "kvhead", None),
        P("seq", "kvhead", None),
        P("seq", "kvhead", None),
        P("kvhead", ("feature", "seq")),
    )
    out_specs = P(("seq", "feature"), "kvhead")

    def local(queries, keys, values, w_out):
        parts, groups = mesh.shape["feature"], mesh.shape["kvhead"]
        body = by_heads if (groups, parts, keys.shape[1]) == (2, 4, parts) else plain
        return body(queries, keys, values, w_out)

    return jax.shard_map(local, mesh=mesh, in_specs=in_specs, out_specs=out_specs, check_vma=False)
```

```python
import functools

import jax
import jax.numpy as jnp
from jax import lax
from jax.experimental import pallas as pl
from jax.experimental.pallas import tpu as pltpu
from jax.sharding import PartitionSpec as P

F32 = jnp.float32
BF16 = jnp.bfloat16
VMEM_LIMIT = 20 * 1024 * 1024
WHOLE = 60 * 1024 * 1024
NT = (((1,), (1,)), ((), ()))


def split(a):
    high = a.astype(BF16)
    return high, (a - high.astype(F32)).astype(BF16)


def mm(a, b):
    return jnp.dot(a, b, preferred_element_type=F32)


def after(*arrays):
    return lax.optimization_barrier(arrays)


def brief(micros=0):
    return pl.CostEstimate(flops=1 + micros * 10**9, bytes_accessed=1, transcendentals=0)


def params(limit=VMEM_LIMIT):
    return pltpu.CompilerParams(vmem_limit_bytes=limit)


def smem():
    return pl.BlockSpec(memory_space=pltpu.SMEM)


def vmem(n):
    return [pl.BlockSpec(memory_space=pltpu.VMEM)] * n


def ring_at(place, n):
    half = (n + 1) // 2
    return jnp.where(place < half, 2 * place, 2 * (n - place) - 1)


def ring_place(index, n):
    return jnp.where(index % 2 == 0, index // 2, n - 1 - index // 2)


def ring_perm(n, step):
    order = list(range(0, n, 2)) + list(range(1, n, 2))[::-1]
    return [(order[i], order[(i + step) % n]) for i in range(n)]


def prepare_keys(pairs):
    n = len(pairs)
    _, rows, d = pairs[0].shape

    def kernel(*refs):
        kt, vv, held, sems = refs[n:]
        copies = [pltpu.make_async_copy(refs[j], held.at[j], sems.at[j]) for j in range(n)]
        for copy in copies:
            copy.start()
        for j in range(n):
            copies[j].wait()
            at = pl.ds(j * rows, rows)
            k_high, k_low = split(held[j, 0].T)
            kt[0:d, at] = k_high
            kt[d : 2 * d, at] = k_high
            kt[2 * d : 3 * d, at] = k_low
            v_high, v_low = split(held[j, 1])
            upper, lower = pl.ds(2 * j * rows, rows), pl.ds((2 * j + 1) * rows, rows)
            vv[upper, 0:d] = v_high
            vv[upper, d : 2 * d] = v_low
            vv[lower, 0:d] = v_high
            vv[lower, d : 2 * d] = jnp.zeros((rows, d), BF16)

    return pl.pallas_call(
        kernel,
        out_shape=(
            jax.ShapeDtypeStruct((3 * d, n * rows), BF16),
            jax.ShapeDtypeStruct((2 * n * rows, 2 * d), BF16),
        ),
        in_specs=[pl.BlockSpec(memory_space=pltpu.MemorySpace.HBM)] * n,
        out_specs=tuple(vmem(2)),
        scratch_shapes=[pltpu.VMEM((n, 2, rows, d), F32), pltpu.SemaphoreType.DMA((n,))],
        compiler_params=params(WHOLE),
        cost_estimate=brief(0),
        name="prepare_keys",
    )(*pairs)


def attend(meta, heads, slot, kt, vv):
    _, rows, d = heads[0].shape
    group = sum(part.shape[0] for part in heads)
    count = kt.shape[1] // rows
    n = len(heads)
    scale = d ** (-0.5)

    def kernel(meta_ref, *refs):
        kt_ref, vv_ref, out, parts, acc, den = refs[n:]
        shape = (rows, rows)
        keep = lax.broadcasted_iota(jnp.int32, shape, 1) <= lax.broadcasted_iota(jnp.int32, shape, 0)

        def chunk(j, own):
            for h in range(group):
                at = pl.ds(h * rows, rows)
                scores = mm(parts[at], kt_ref[:, pl.ds(j * rows, rows)])
                squared = scores * scores
                if own:
                    squared = jnp.where(keep, squared, 0.0)
                high, low = split(squared)
                both = mm(jnp.concatenate([high, low], axis=1), vv_ref[pl.ds(2 * j * rows, 2 * rows)])
                total = jnp.broadcast_to(jnp.sum(squared, axis=1, keepdims=True), (rows, d))
                if own:
                    acc[at], den[at] = both, total
                else:
                    acc[at] += both
                    den[at] += total

        start = 0
        for ref in refs[:n]:
            m = ref.shape[0] * rows
            at = pl.ds(start, m)
            high, low = split(ref[...].reshape(m, d) * scale)
            parts[at, 0:d] = high
            parts[at, d : 2 * d] = low
            parts[at, 2 * d : 3 * d] = high
            start += m
        chunk(slot, True)
        for j in range(count):
            if j != slot:
                pl.when(meta_ref[j] < meta_ref[slot])(functools.partial(chunk, j, False))
        for h in range(group):
            at = pl.ds(h * rows, rows)
            numerator = acc[at, 0:d] + acc[at, d : 2 * d]
            out[:, h * d : (h + 1) * d] = numerator / (den[at] + 1.0)

    return pl.pallas_call(
        kernel,
        out_shape=jax.ShapeDtypeStruct((rows, group * d), F32),
        in_specs=[smem()] + vmem(n + 2),
        out_specs=vmem(1)[0],
        scratch_shapes=[
            pltpu.VMEM((group * rows, 3 * d), BF16),
            pltpu.VMEM((group * rows, 2 * d), F32),
            pltpu.VMEM((group * rows, d), F32),
        ],
        compiler_params=params(WHOLE),
        cost_estimate=brief(),
        name="attend",
    )(meta, *heads, kt, vv)


def prepare_weights(meta, pieces):
    n = len(pieces)
    columns, k = pieces[0].shape

    def kernel(meta_ref, *refs):
        high, low = refs[n:]
        for i in range(n):
            at = pl.ds(pl.multiple_of(meta_ref[2 * i + 1] * columns, 16), columns)
            w_high, w_low = split(refs[i][...])
            high[meta_ref[2 * i], at] = w_high
            low[meta_ref[2 * i], at] = w_low

    shape = jax.ShapeDtypeStruct((2, n // 2 * columns, k), BF16)
    return pl.pallas_call(
        kernel,
        out_shape=(shape, shape),
        in_specs=[smem()] + vmem(n),
        out_specs=tuple(vmem(2)),
        compiler_params=params(),
        cost_estimate=brief(),
        name="prepare_weights",
    )(meta, *pieces)


def project(blocks, high, low, half, chunks):
    n = len(blocks)
    rows = n * blocks[0].shape[0]
    columns = high.shape[1]
    ends = [-(-rows * i // (16 * chunks)) * 16 for i in range(chunks + 1)]

    def kernel(*refs):
        high_ref, low_ref = refs[n : n + 2]
        a_high, a_low = split(jnp.concatenate([ref[...] for ref in refs[:n]], axis=0))
        dot = functools.partial(lax.dot_general, dimension_numbers=NT, preferred_element_type=F32)
        w_high = high_ref[half]
        total = dot(a_high, w_high) + dot(a_low, w_high) + dot(a_high, low_ref[half])
        for i, ref in enumerate(refs[n + 2 :]):
            ref[...] = total[ends[i] : ends[i + 1]]

    return pl.pallas_call(
        kernel,
        out_shape=tuple(
            jax.ShapeDtypeStruct((b - a, columns), F32) for a, b in zip(ends, ends[1:])
        ),
        in_specs=vmem(n + 2),
        out_specs=tuple(vmem(chunks)),
        compiler_params=params(),
        cost_estimate=brief(),
        name="project",
    )(*blocks, high, low)


def fold(meta, kept, got, blocks, order):
    rows = kept.shape[0] // blocks
    cut = rows // sum(len(group) for group in order)
    columns = kept.shape[1]
    n = len(got)

    def kernel(meta_ref, kept_ref, *refs):
        outs, total = refs[n:-1], refs[-1]
        start = 0
        for ref in refs[:n]:
            at = pl.ds(start, ref.shape[0])
            total[at] = kept_ref[at] + ref[...]
            start += ref.shape[0]
        for out, group in zip(outs, order):
            for i, e in enumerate(group):
                for b in range(blocks):
                    out[i, b] = total[pl.ds(pl.multiple_of(b * rows + (meta_ref[0] ^ e) * cut, 8), cut)]

    return pl.pallas_call(
        kernel,
        out_shape=tuple(
            jax.ShapeDtypeStruct((len(group), blocks, cut, columns), F32) for group in order
        ),
        in_specs=[smem()] + vmem(1 + n),
        out_specs=tuple(vmem(len(order))),
        scratch_shapes=[pltpu.VMEM((blocks * rows, columns), F32)],
        compiler_params=params(),
        cost_estimate=brief(),
        name="fold",
    )(meta, kept, *got)


def assemble(meta, parts, halves):
    n = len(parts)
    rows, columns = parts[0].shape
    width = columns // halves

    def kernel(meta_ref, *refs):
        out, held = refs[n:]
        for j in range(n):
            held[meta_ref[j]] = refs[j][...]
        pieces = [
            held[z][:, h * width : (h + 1) * width] for h in range(halves) for z in range(n)
        ]
        out[...] = jnp.concatenate(pieces, axis=1)

    return pl.pallas_call(
        kernel,
        out_shape=jax.ShapeDtypeStruct((rows, n * columns), F32),
        in_specs=[smem()] + vmem(n),
        out_specs=vmem(1)[0],
        scratch_shapes=[pltpu.VMEM((n, rows, columns), F32)],
        compiler_params=params(),
        cost_estimate=brief(),
        name="assemble",
    )(meta, *parts)


def by_heads(queries, keys, values, w_out):
    rows, local_heads, d = queries.shape
    kv_local = keys.shape[1]
    group = local_heads // kv_local
    parts, planes = lax.axis_size("feature"), lax.axis_size("seq")
    f, c, s = (lax.axis_index(a) for a in ("feature", "kvhead", "seq"))
    at = ring_place(s, planes)
    ints = lambda *xs: jnp.stack([jnp.asarray(x, jnp.int32) for x in xs])
    held = [ring_at((at - j) % planes, planes) for j in range(planes)]
    sender = [ring_at((at + j) % planes, planes) for j in range(planes)]

    ring = lambda x, step: lax.ppermute(x, "seq", ring_perm(planes, step))
    swap = lambda x: lax.ppermute(x, "kvhead", [(0, 1), (1, 0)])

    kv = jnp.stack([lax.dynamic_index_in_dim(a, f, 1, False) for a in (keys, values)])
    pairs = [ring(kv, j) if j else kv for j in range(planes)]

    k_rows = group * d
    half = parts // 2
    turn = lambda x: lax.dynamic_slice_in_dim(w_out, x * k_rows, k_rows, 0).T
    cross = lambda x, e: lax.ppermute(x, "feature", [(i, i ^ e) for i in range(parts)])
    pieces = [cross(turn(f ^ e), e) for e in range(1, parts)]
    places = []
    for e in range(parts):
        places += [jnp.where((f ^ e) // half == c, 0, 1), (f ^ e) % half]

    q = lax.dynamic_slice_in_dim(queries, f * group, group, 1).transpose(1, 0, 2)
    *pairs, mine, meta, place, upper, lower = after(
        *pairs, turn(f), ints(*held), ints(f), q[: group // 2], q[group // 2 :]
    )
    sent = [ring(upper, 1), ring(lower, 1)]
    kt, vv = prepare_keys(pairs)
    owns = {0: attend(meta, [upper, lower], 0, kt, vv)}
    back, *sent = after(owns[0], *sent)
    owns[planes - 1] = ring(back, -1)
    sent[0], sent[1], *pieces = after(*sent, *pieces)
    owns[1] = attend(meta, sent, 1, kt, vv)
    owns[2] = ring(owns[1], 1)
    high, low = prepare_weights(ints(*places), [mine] + pieces)

    exchange = lambda xs: [swap(x) for x in xs]
    single = tuple((e,) for e in range(parts))
    both = [owns[0], owns[1]]
    given = exchange(project(both, high, low, 1, 4))
    (kept,) = project(both, high, low, 0, 1)
    owns[3], *given = after(owns[3], *given)
    keep_a, send_a = fold(place, kept, given, 2, ((0, 2), (1, 3)))
    owns[3], keep_a, send_a = after(owns[3], keep_a, send_a)
    got_a = cross(send_a, 1)
    given = exchange(project([owns[3]], high, low, 1, 3))
    (kept,) = project([owns[3]], high, low, 0, 1)
    keep_b, send_b = fold(place, kept, given, 1, ((0, 1), (2, 3)))
    got_b = cross(send_b, 2)
    owns[2], got_a, got_b = after(owns[2], got_a, got_b)
    given = exchange(project([owns[2]], high, low, 1, 2))
    (kept,) = project([owns[2]], high, low, 0, 1)
    keep_a, keep_b = keep_a + got_a, keep_b + got_b
    keep_c, *send_c = fold(place, kept, given, 1, single)
    got_a, got_b = cross(keep_a[1], 2), cross(keep_b[1], 1)
    total_a, total_b = keep_a[0] + got_a, keep_b[0] + got_b
    total = keep_c
    for e, x in enumerate(send_c):
        total = total + cross(x, e + 1)
    results = [total_a[0], ring(total_a[1], -1), ring(total[0, 0], -2), ring(total_b[0], -3)]
    return assemble(ints(*sender), [results[j] for j in range(planes)], half)


def plain(queries, keys, values, w_out):
    highest = lax.Precision.HIGHEST
    rows, local_heads, d = queries.shape
    kv_local = keys.shape[1]
    parts, planes = lax.axis_size("feature"), lax.axis_size("seq")
    f, c, s = (lax.axis_index(a) for a in ("feature", "kvhead", "seq"))
    cut = rows // parts
    q = lax.dynamic_slice_in_dim(queries, f * cut, cut, 0) * d ** (-0.5)
    q = q.reshape(cut, kv_local, local_heads // kv_local, d)
    k = lax.all_gather(keys, "seq", axis=0, tiled=True)
    v = lax.all_gather(values, "seq", axis=0, tiled=True)
    scores = jnp.einsum("tkgd,skd->kgts", q, k, precision=highest)
    row = s * rows + f * cut + jnp.arange(cut)
    allowed = jnp.arange(k.shape[0])[None, :] <= row[:, None]
    squared = jnp.where(allowed, scores * scores, 0.0)
    numerator = jnp.einsum("kgts,skd->tkgd", squared, v, precision=highest)
    denominator = jnp.transpose(jnp.sum(squared, axis=-1), (2, 0, 1))
    attended = (numerator / (denominator[..., None] + 1.0)).reshape(cut, local_heads * d)
    attended = lax.all_gather(attended, ("seq", "feature"), axis=0, tiled=True)
    partial = jnp.dot(attended, w_out, precision=highest, preferred_element_type=F32)
    whole = lax.psum(partial, "kvhead")
    mine = lax.all_to_all(whole, ("seq", "feature"), 0, 1, tiled=True)
    columns = w_out.shape[1]
    mine = mine.reshape(cut, planes, parts, columns).transpose(0, 2, 1, 3).reshape(cut, -1)
    width = mine.shape[1] // lax.axis_size("kvhead")
    return lax.dynamic_slice_in_dim(mine, c * width, width, 1)


def solution(mesh):
    in_specs = (
        P("seq", "kvhead", None),
        P("seq", "kvhead", None),
        P("seq", "kvhead", None),
        P("kvhead", ("feature", "seq")),
    )
    out_specs = P(("seq", "feature"), "kvhead")

    def local(queries, keys, values, w_out):
        parts, groups = mesh.shape["feature"], mesh.shape["kvhead"]
        body = by_heads if (groups, parts, keys.shape[1]) == (2, 4, parts) else plain
        return body(queries, keys, values, w_out)

    return jax.shard_map(local, mesh=mesh, in_specs=in_specs, out_specs=out_specs, check_vma=False)
```

```python
import functools

import jax
import jax.numpy as jnp
from jax import lax
from jax.experimental import pallas as pl
from jax.experimental.pallas import tpu as pltpu
from jax.sharding import PartitionSpec as P

F32 = jnp.float32
BF16 = jnp.bfloat16
VMEM_LIMIT = 20 * 1024 * 1024
WHOLE = 63 * 1024 * 1024
NT = (((1,), (1,)), ((), ()))


def split(a):
    high = a.astype(BF16)
    return high, (a - high.astype(F32)).astype(BF16)


def mm(a, b):
    return jnp.dot(a, b, preferred_element_type=F32)


def after(*arrays):
    return lax.optimization_barrier(arrays)


def brief(micros=0):
    return pl.CostEstimate(flops=1 + micros * 10**9, bytes_accessed=1, transcendentals=0)


def params(limit=VMEM_LIMIT):
    return pltpu.CompilerParams(vmem_limit_bytes=limit)


def smem():
    return pl.BlockSpec(memory_space=pltpu.SMEM)


def vmem(n):
    return [pl.BlockSpec(memory_space=pltpu.VMEM)] * n


def ring_at(place, n):
    half = (n + 1) // 2
    return jnp.where(place < half, 2 * place, 2 * (n - place) - 1)


def ring_place(index, n):
    return jnp.where(index % 2 == 0, index // 2, n - 1 - index // 2)


def ring_perm(n, step):
    order = list(range(0, n, 2)) + list(range(1, n, 2))[::-1]
    return [(order[i], order[(i + step) % n]) for i in range(n)]


def prepare_keys(pairs):
    n = len(pairs)
    _, rows, d = pairs[0].shape

    def kernel(*refs):
        kt, vv, held, sems = refs[n:]
        copies = [pltpu.make_async_copy(refs[j], held.at[j], sems.at[j]) for j in range(n)]
        for copy in copies:
            copy.start()
        for j in range(n):
            copies[j].wait()
            at = pl.ds(j * rows, rows)
            k_high, k_low = split(held[j, 0].T)
            kt[0:d, at] = k_high
            kt[d : 2 * d, at] = k_high
            kt[2 * d : 3 * d, at] = k_low
            v_high, v_low = split(held[j, 1])
            upper, lower = pl.ds(2 * j * rows, rows), pl.ds((2 * j + 1) * rows, rows)
            vv[upper, 0:d] = v_high
            vv[upper, d : 2 * d] = v_low
            vv[lower, 0:d] = v_high
            vv[lower, d : 2 * d] = jnp.zeros((rows, d), BF16)

    return pl.pallas_call(
        kernel,
        out_shape=(
            jax.ShapeDtypeStruct((3 * d, n * rows), BF16),
            jax.ShapeDtypeStruct((2 * n * rows, 2 * d), BF16),
        ),
        in_specs=[pl.BlockSpec(memory_space=pltpu.MemorySpace.HBM)] * n,
        out_specs=tuple(vmem(2)),
        scratch_shapes=[pltpu.VMEM((n, 2, rows, d), F32), pltpu.SemaphoreType.DMA((n,))],
        compiler_params=params(WHOLE),
        cost_estimate=brief(0),
        name="prepare_keys",
    )(*pairs)


def attend(meta, heads, slot, kt, vv):
    _, rows, d = heads[0].shape
    group = sum(part.shape[0] for part in heads)
    count = kt.shape[1] // rows
    n = len(heads)
    scale = d ** (-0.5)

    def kernel(meta_ref, *refs):
        kt_ref, vv_ref, out, parts, acc, den = refs[n:]
        shape = (rows, rows)
        keep = lax.broadcasted_iota(jnp.int32, shape, 1) <= lax.broadcasted_iota(jnp.int32, shape, 0)

        def chunk(j, own):
            for h in range(group):
                at = pl.ds(h * rows, rows)
                scores = mm(parts[at], kt_ref[:, pl.ds(j * rows, rows)])
                squared = scores * scores
                if own:
                    squared = jnp.where(keep, squared, 0.0)
                high, low = split(squared)
                both = mm(jnp.concatenate([high, low], axis=1), vv_ref[pl.ds(2 * j * rows, 2 * rows)])
                total = jnp.broadcast_to(jnp.sum(squared, axis=1, keepdims=True), (rows, d))
                if own:
                    acc[at], den[at] = both, total
                else:
                    acc[at] += both
                    den[at] += total

        start = 0
        for ref in refs[:n]:
            m = ref.shape[0] * rows
            at = pl.ds(start, m)
            high, low = split(ref[...].reshape(m, d) * scale)
            parts[at, 0:d] = high
            parts[at, d : 2 * d] = low
            parts[at, 2 * d : 3 * d] = high
            start += m
        chunk(slot, True)
        for j in range(count):
            if j != slot:
                pl.when(meta_ref[j] < meta_ref[slot])(functools.partial(chunk, j, False))
        for h in range(group):
            at = pl.ds(h * rows, rows)
            numerator = acc[at, 0:d] + acc[at, d : 2 * d]
            out[:, h * d : (h + 1) * d] = numerator / (den[at] + 1.0)

    return pl.pallas_call(
        kernel,
        out_shape=jax.ShapeDtypeStruct((rows, group * d), F32),
        in_specs=[smem()] + vmem(n + 2),
        out_specs=vmem(1)[0],
        scratch_shapes=[
            pltpu.VMEM((group * rows, 3 * d), BF16),
            pltpu.VMEM((group * rows, 2 * d), F32),
            pltpu.VMEM((group * rows, d), F32),
        ],
        compiler_params=params(WHOLE),
        cost_estimate=brief(),
        name="attend",
    )(meta, *heads, kt, vv)


def prepare_weights(meta, pieces):
    n = len(pieces)
    columns, k = pieces[0].shape

    def kernel(meta_ref, *refs):
        high, low, held, sem = refs[n:]
        copy = pltpu.make_async_copy(refs[0], held, sem)
        copy.start()
        for i in list(range(1, n)) + [0]:
            if i == 0:
                copy.wait()
            at = pl.ds(pl.multiple_of(meta_ref[2 * i + 1] * columns, 16), columns)
            w_high, w_low = split(refs[i][...] if i else held[...])
            high[meta_ref[2 * i], at] = w_high
            low[meta_ref[2 * i], at] = w_low

    shape = jax.ShapeDtypeStruct((2, n // 2 * columns, k), BF16)
    return pl.pallas_call(
        kernel,
        out_shape=(shape, shape),
        in_specs=[smem(), pl.BlockSpec(memory_space=pltpu.MemorySpace.HBM)] + vmem(n - 1),
        out_specs=tuple(vmem(2)),
        scratch_shapes=[pltpu.VMEM((columns, k), F32), pltpu.SemaphoreType.DMA],
        compiler_params=params(),
        cost_estimate=brief(),
        name="prepare_weights",
    )(meta, *pieces)


def project(blocks, high, low, half, chunks):
    n = len(blocks)
    rows = n * blocks[0].shape[0]
    columns = high.shape[1]
    ends = [-(-rows * i // (16 * chunks)) * 16 for i in range(chunks + 1)]

    def kernel(*refs):
        high_ref, low_ref = refs[n : n + 2]
        a_high, a_low = split(jnp.concatenate([ref[...] for ref in refs[:n]], axis=0))
        dot = functools.partial(lax.dot_general, dimension_numbers=NT, preferred_element_type=F32)
        w_high = high_ref[half]
        total = dot(a_high, w_high) + dot(a_low, w_high) + dot(a_high, low_ref[half])
        for i, ref in enumerate(refs[n + 2 :]):
            ref[...] = total[ends[i] : ends[i + 1]]

    return pl.pallas_call(
        kernel,
        out_shape=tuple(
            jax.ShapeDtypeStruct((b - a, columns), F32) for a, b in zip(ends, ends[1:])
        ),
        in_specs=vmem(n + 2),
        out_specs=tuple(vmem(chunks)),
        compiler_params=params(),
        cost_estimate=brief(),
        name="project",
    )(*blocks, high, low)


def fold(meta, kept, got, blocks, parts, orders):
    rows = kept.shape[0] // blocks
    cut = rows // parts
    half = cut // 2
    columns = kept.shape[1]
    n = len(got)

    def kernel(meta_ref, kept_ref, *refs):
        outs, total = refs[n:-1], refs[-1]
        start = 0
        for ref in refs[:n]:
            at = pl.ds(start, ref.shape[0])
            total[at] = kept_ref[at] + ref[...]
            start += ref.shape[0]
        for out, (side, group) in zip(outs, orders):
            for i, e in enumerate(group):
                for b in range(blocks):
                    start = b * rows + (meta_ref[0] ^ e) * cut + (side or 0) * half
                    out[i, b] = total[pl.ds(pl.multiple_of(start, 8), out.shape[2])]

    return pl.pallas_call(
        kernel,
        out_shape=tuple(
            jax.ShapeDtypeStruct((len(group), blocks, cut if side is None else half, columns), F32)
            for side, group in orders
        ),
        in_specs=[smem()] + vmem(1 + n),
        out_specs=tuple(vmem(len(orders))),
        scratch_shapes=[pltpu.VMEM((blocks * rows, columns), F32)],
        compiler_params=params(),
        cost_estimate=brief(),
        name="fold",
    )(meta, kept, *got)


def assemble(meta, parts, halves):
    n = len(parts)
    rows, columns = parts[0].shape
    width = columns // halves

    def kernel(meta_ref, *refs):
        out, held = refs[n:]
        for j in range(n):
            held[meta_ref[j]] = refs[j][...]
        pieces = [
            held[z][:, h * width : (h + 1) * width] for h in range(halves) for z in range(n)
        ]
        out[...] = jnp.concatenate(pieces, axis=1)

    return pl.pallas_call(
        kernel,
        out_shape=jax.ShapeDtypeStruct((rows, n * columns), F32),
        in_specs=[smem()] + vmem(n),
        out_specs=vmem(1)[0],
        scratch_shapes=[pltpu.VMEM((n, rows, columns), F32)],
        compiler_params=params(),
        cost_estimate=brief(),
        name="assemble",
    )(meta, *parts)


def by_heads(queries, keys, values, w_out):
    rows, local_heads, d = queries.shape
    kv_local = keys.shape[1]
    group = local_heads // kv_local
    parts, planes = lax.axis_size("feature"), lax.axis_size("seq")
    f, c, s = (lax.axis_index(a) for a in ("feature", "kvhead", "seq"))
    at = ring_place(s, planes)
    ints = lambda *xs: jnp.stack([jnp.asarray(x, jnp.int32) for x in xs])
    held = [ring_at((at - j) % planes, planes) for j in range(planes)]
    sender = [ring_at((at + j) % planes, planes) for j in range(planes)]

    ring = lambda x, step: lax.ppermute(x, "seq", ring_perm(planes, step))
    swap = lambda x: lax.ppermute(x, "kvhead", [(0, 1), (1, 0)])

    kv = jnp.stack([lax.dynamic_index_in_dim(a, f, 1, False) for a in (keys, values)])
    pairs = [ring(kv, j) if j else kv for j in range(planes)]

    k_rows = group * d
    half = parts // 2
    turn = lambda x: lax.dynamic_slice_in_dim(w_out, x * k_rows, k_rows, 0).T
    cross = lambda x, e: lax.ppermute(x, "feature", [(i, i ^ e) for i in range(parts)])
    pieces = [cross(turn(f ^ e), e) for e in range(1, parts)]
    places = []
    for e in range(parts):
        places += [jnp.where((f ^ e) // half == c, 0, 1), (f ^ e) % half]

    q = lax.dynamic_slice_in_dim(queries, f * group, group, 1).transpose(1, 0, 2)
    *pairs, mine, meta, place, upper, lower = after(
        *pairs, turn(f), ints(*held), ints(f), q[: group // 2], q[group // 2 :]
    )
    sent = [ring(upper, 1), ring(lower, 1)]
    kt, vv = prepare_keys(pairs)
    owns = {0: attend(meta, [upper, lower], 0, kt, vv)}
    back, *sent = after(owns[0], *sent)
    owns[planes - 1] = ring(back, -1)
    sent[0], sent[1], *pieces = after(*sent, *pieces)
    owns[1] = attend(meta, sent, 1, kt, vv)
    owns[2] = ring(owns[1], 1)
    high, low = prepare_weights(ints(*places), [mine] + pieces)

    exchange = lambda xs: [swap(x) for x in xs]
    both = [owns[0], owns[1]]
    given = exchange(project(both, high, low, 1, 4))
    (kept,) = project(both, high, low, 0, 1)
    owns[3], *given = after(owns[3], *given)
    orders = ((0, (0, 2)), (1, (0, 1)), (0, (1, 3)), (1, (2, 3)))
    add = lambda xs, ys: [x + y for x, y in zip(xs, ys)]
    first = lambda sends: [cross(sends[0], 1), cross(sends[1], 2)]
    second = lambda xs: [cross(xs[0][1], 2), cross(xs[1][1], 1)]
    join = lambda xs, ys: jnp.concatenate([x[0] + y for x, y in zip(xs, ys)], axis=1)
    *keep_a, up, down = fold(place, kept, given, 2, parts, orders)
    owns[3], up, down, *keep_a = after(owns[3], up, down, *keep_a)
    got_a = first([up, down])
    given = exchange(project([owns[3]], high, low, 1, 3))
    (kept,) = project([owns[3]], high, low, 0, 1)
    kept, *got_a = after(kept, *got_a)
    keep_a = add(keep_a, got_a)
    *keep_b, up, down = fold(place, kept, given, 1, parts, orders)
    got_b = first([up, down])
    owns[2], *got_b = after(owns[2], *got_b)
    keep_b = add(keep_b, got_b)
    given = exchange(project([owns[2]], high, low, 1, 2))
    (kept,) = project([owns[2]], high, low, 0, 1)
    *keep_c, up, down = fold(place, kept, given, 1, parts, orders)
    got_a = second(keep_a)
    got_b = second(keep_b)
    *got, _, _ = after(*got_a, *got_b, up, down)
    got_a, got_b = got[: len(got_a)], got[len(got_a) :]
    total_a = join(keep_a, got_a)
    total_b = join(keep_b, got_b)
    keep_c = add(keep_c, first([up, down]))
    total = join(keep_c, second(keep_c))
    results = [total_a[0], ring(total_a[1], -1), ring(total[0], -2), ring(total_b[0], -3)]
    return assemble(ints(*sender), [results[j] for j in range(planes)], half)


def plain(queries, keys, values, w_out):
    highest = lax.Precision.HIGHEST
    rows, local_heads, d = queries.shape
    kv_local = keys.shape[1]
    parts, planes = lax.axis_size("feature"), lax.axis_size("seq")
    f, c, s = (lax.axis_index(a) for a in ("feature", "kvhead", "seq"))
    cut = rows // parts
    q = lax.dynamic_slice_in_dim(queries, f * cut, cut, 0) * d ** (-0.5)
    q = q.reshape(cut, kv_local, local_heads // kv_local, d)
    k = lax.all_gather(keys, "seq", axis=0, tiled=True)
    v = lax.all_gather(values, "seq", axis=0, tiled=True)
    scores = jnp.einsum("tkgd,skd->kgts", q, k, precision=highest)
    row = s * rows + f * cut + jnp.arange(cut)
    allowed = jnp.arange(k.shape[0])[None, :] <= row[:, None]
    squared = jnp.where(allowed, scores * scores, 0.0)
    numerator = jnp.einsum("kgts,skd->tkgd", squared, v, precision=highest)
    denominator = jnp.transpose(jnp.sum(squared, axis=-1), (2, 0, 1))
    attended = (numerator / (denominator[..., None] + 1.0)).reshape(cut, local_heads * d)
    attended = lax.all_gather(attended, ("seq", "feature"), axis=0, tiled=True)
    partial = jnp.dot(attended, w_out, precision=highest, preferred_element_type=F32)
    whole = lax.psum(partial, "kvhead")
    mine = lax.all_to_all(whole, ("seq", "feature"), 0, 1, tiled=True)
    columns = w_out.shape[1]
    mine = mine.reshape(cut, planes, parts, columns).transpose(0, 2, 1, 3).reshape(cut, -1)
    width = mine.shape[1] // lax.axis_size("kvhead")
    return lax.dynamic_slice_in_dim(mine, c * width, width, 1)


def solution(mesh):
    in_specs = (
        P("seq", "kvhead", None),
        P("seq", "kvhead", None),
        P("seq", "kvhead", None),
        P("kvhead", ("feature", "seq")),
    )
    out_specs = P(("seq", "feature"), "kvhead")

    def local(queries, keys, values, w_out):
        parts, groups = mesh.shape["feature"], mesh.shape["kvhead"]
        body = by_heads if (groups, parts, keys.shape[1]) == (2, 4, parts) else plain
        return body(queries, keys, values, w_out)

    return jax.shard_map(local, mesh=mesh, in_specs=in_specs, out_specs=out_specs, check_vma=False)
```

```python
import functools

import jax
import jax.numpy as jnp
from jax import lax
from jax.experimental import pallas as pl
from jax.experimental.pallas import tpu as pltpu
from jax.sharding import PartitionSpec as P

F32 = jnp.float32
BF16 = jnp.bfloat16
VMEM_LIMIT = 20 * 1024 * 1024
WHOLE = 63 * 1024 * 1024
NT = (((1,), (1,)), ((), ()))


def split(a):
    high = a.astype(BF16)
    return high, (a - high.astype(F32)).astype(BF16)


def mm(a, b):
    return jnp.dot(a, b, preferred_element_type=F32)


def after(*arrays):
    return lax.optimization_barrier(arrays)


def brief(micros=0):
    return pl.CostEstimate(flops=1 + micros * 10**9, bytes_accessed=1, transcendentals=0)


def params(limit=VMEM_LIMIT):
    return pltpu.CompilerParams(vmem_limit_bytes=limit)


def smem():
    return pl.BlockSpec(memory_space=pltpu.SMEM)


def vmem(n):
    return [pl.BlockSpec(memory_space=pltpu.VMEM)] * n


def ring_at(place, n):
    half = (n + 1) // 2
    return jnp.where(place < half, 2 * place, 2 * (n - place) - 1)


def ring_place(index, n):
    return jnp.where(index % 2 == 0, index // 2, n - 1 - index // 2)


def ring_perm(n, step):
    order = list(range(0, n, 2)) + list(range(1, n, 2))[::-1]
    return [(order[i], order[(i + step) % n]) for i in range(n)]


def prepare_keys(pairs):
    n = len(pairs)
    _, rows, d = pairs[0].shape

    def kernel(*refs):
        kt, vv, held, sems = refs[n:]
        copies = [pltpu.make_async_copy(refs[j], held.at[j], sems.at[j]) for j in range(n)]
        for copy in copies:
            copy.start()
        for j in range(n):
            copies[j].wait()
            at = pl.ds(j * rows, rows)
            k_high, k_low = split(held[j, 0].T)
            kt[0:d, at] = k_high
            kt[d : 2 * d, at] = k_high
            kt[2 * d : 3 * d, at] = k_low
            v_high, v_low = split(held[j, 1])
            upper, lower = pl.ds(2 * j * rows, rows), pl.ds((2 * j + 1) * rows, rows)
            vv[upper, 0:d] = v_high
            vv[upper, d : 2 * d] = v_low
            vv[lower, 0:d] = v_high
            vv[lower, d : 2 * d] = jnp.zeros((rows, d), BF16)

    return pl.pallas_call(
        kernel,
        out_shape=(
            jax.ShapeDtypeStruct((3 * d, n * rows), BF16),
            jax.ShapeDtypeStruct((2 * n * rows, 2 * d), BF16),
        ),
        in_specs=[pl.BlockSpec(memory_space=pltpu.MemorySpace.HBM)] * n,
        out_specs=tuple(vmem(2)),
        scratch_shapes=[pltpu.VMEM((n, 2, rows, d), F32), pltpu.SemaphoreType.DMA((n,))],
        compiler_params=params(WHOLE),
        cost_estimate=brief(0),
        name="prepare_keys",
    )(*pairs)


def attend(meta, heads, slot, kt, vv):
    _, rows, d = heads[0].shape
    group = sum(part.shape[0] for part in heads)
    count = kt.shape[1] // rows
    n = len(heads)
    scale = d ** (-0.5)

    def kernel(meta_ref, *refs):
        kt_ref, vv_ref, out, parts, acc, den = refs[n:]
        shape = (rows, rows)
        keep = lax.broadcasted_iota(jnp.int32, shape, 1) <= lax.broadcasted_iota(jnp.int32, shape, 0)

        def chunk(j, own):
            for h in range(group):
                at = pl.ds(h * rows, rows)
                scores = mm(parts[at], kt_ref[:, pl.ds(j * rows, rows)])
                squared = scores * scores
                if own:
                    squared = jnp.where(keep, squared, 0.0)
                high, low = split(squared)
                both = mm(jnp.concatenate([high, low], axis=1), vv_ref[pl.ds(2 * j * rows, 2 * rows)])
                total = jnp.broadcast_to(jnp.sum(squared, axis=1, keepdims=True), (rows, d))
                if own:
                    acc[at], den[at] = both, total
                else:
                    acc[at] += both
                    den[at] += total

        start = 0
        for ref in refs[:n]:
            m = ref.shape[0] * rows
            at = pl.ds(start, m)
            high, low = split(ref[...].reshape(m, d) * scale)
            parts[at, 0:d] = high
            parts[at, d : 2 * d] = low
            parts[at, 2 * d : 3 * d] = high
            start += m
        chunk(slot, True)
        for j in range(count):
            if j != slot:
                pl.when(meta_ref[j] < meta_ref[slot])(functools.partial(chunk, j, False))
        for h in range(group):
            at = pl.ds(h * rows, rows)
            numerator = acc[at, 0:d] + acc[at, d : 2 * d]
            out[:, h * d : (h + 1) * d] = numerator / (den[at] + 1.0)

    return pl.pallas_call(
        kernel,
        out_shape=jax.ShapeDtypeStruct((rows, group * d), F32),
        in_specs=[smem()] + vmem(n + 2),
        out_specs=vmem(1)[0],
        scratch_shapes=[
            pltpu.VMEM((group * rows, 3 * d), BF16),
            pltpu.VMEM((group * rows, 2 * d), F32),
            pltpu.VMEM((group * rows, d), F32),
        ],
        compiler_params=params(WHOLE),
        cost_estimate=brief(),
        name="attend",
    )(meta, *heads, kt, vv)


def prepare_weights(meta, pieces):
    n = len(pieces)
    columns, k = pieces[0].shape

    def kernel(meta_ref, *refs):
        high, low, held, sem = refs[n:]
        copy = pltpu.make_async_copy(refs[0], held, sem)
        copy.start()
        for i in list(range(1, n)) + [0]:
            if i == 0:
                copy.wait()
            at = pl.ds(pl.multiple_of(meta_ref[2 * i + 1] * columns, 16), columns)
            w_high, w_low = split(refs[i][...] if i else held[...])
            high[meta_ref[2 * i], at] = w_high
            low[meta_ref[2 * i], at] = w_low

    shape = jax.ShapeDtypeStruct((2, n // 2 * columns, k), BF16)
    return pl.pallas_call(
        kernel,
        out_shape=(shape, shape),
        in_specs=[smem(), pl.BlockSpec(memory_space=pltpu.MemorySpace.HBM)] + vmem(n - 1),
        out_specs=tuple(vmem(2)),
        scratch_shapes=[pltpu.VMEM((columns, k), F32), pltpu.SemaphoreType.DMA],
        compiler_params=params(),
        cost_estimate=brief(),
        name="prepare_weights",
    )(meta, *pieces)


def project(blocks, high, low, half, chunks):
    n = len(blocks)
    rows = n * blocks[0].shape[0]
    columns = high.shape[1]
    ends = [-(-rows * i // (16 * chunks)) * 16 for i in range(chunks + 1)]

    def kernel(*refs):
        high_ref, low_ref = refs[n : n + 2]
        a_high, a_low = split(jnp.concatenate([ref[...] for ref in refs[:n]], axis=0))
        dot = functools.partial(lax.dot_general, dimension_numbers=NT, preferred_element_type=F32)
        w_high = high_ref[half]
        total = dot(a_high, w_high) + dot(a_low, w_high) + dot(a_high, low_ref[half])
        for i, ref in enumerate(refs[n + 2 :]):
            ref[...] = total[ends[i] : ends[i + 1]]

    return pl.pallas_call(
        kernel,
        out_shape=tuple(
            jax.ShapeDtypeStruct((b - a, columns), F32) for a, b in zip(ends, ends[1:])
        ),
        in_specs=vmem(n + 2),
        out_specs=tuple(vmem(chunks)),
        compiler_params=params(),
        cost_estimate=brief(),
        name="project",
    )(*blocks, high, low)


def fold(meta, kept, got, blocks, parts, orders):
    rows = kept.shape[0] // blocks
    cut = rows // parts
    half = cut // 2
    columns = kept.shape[1]
    n = len(got)

    def kernel(meta_ref, kept_ref, *refs):
        outs, total = refs[n:-1], refs[-1]
        start = 0
        for ref in refs[:n]:
            at = pl.ds(start, ref.shape[0])
            total[at] = kept_ref[at] + ref[...]
            start += ref.shape[0]
        for out, (side, group) in zip(outs, orders):
            for i, e in enumerate(group):
                for b in range(blocks):
                    start = b * rows + (meta_ref[0] ^ e) * cut + (side or 0) * half
                    out[i, b] = total[pl.ds(pl.multiple_of(start, 8), out.shape[2])]

    return pl.pallas_call(
        kernel,
        out_shape=tuple(
            jax.ShapeDtypeStruct((len(group), blocks, cut if side is None else half, columns), F32)
            for side, group in orders
        ),
        in_specs=[smem()] + vmem(1 + n),
        out_specs=tuple(vmem(len(orders))),
        scratch_shapes=[pltpu.VMEM((blocks * rows, columns), F32)],
        compiler_params=params(),
        cost_estimate=brief(),
        name="fold",
    )(meta, kept, *got)


def assemble(meta, parts, halves):
    n = len(parts)
    rows, columns = parts[0].shape
    width = columns // halves

    def kernel(meta_ref, *refs):
        out, held = refs[n:]
        for j in range(n):
            held[meta_ref[j]] = refs[j][...]
        pieces = [
            held[z][:, h * width : (h + 1) * width] for h in range(halves) for z in range(n)
        ]
        out[...] = jnp.concatenate(pieces, axis=1)

    return pl.pallas_call(
        kernel,
        out_shape=jax.ShapeDtypeStruct((rows, n * columns), F32),
        in_specs=[smem()] + vmem(n),
        out_specs=vmem(1)[0],
        scratch_shapes=[pltpu.VMEM((n, rows, columns), F32)],
        compiler_params=params(),
        cost_estimate=brief(),
        name="assemble",
    )(meta, *parts)


def by_heads(queries, keys, values, w_out):
    rows, local_heads, d = queries.shape
    kv_local = keys.shape[1]
    group = local_heads // kv_local
    parts, planes = lax.axis_size("feature"), lax.axis_size("seq")
    f, c, s = (lax.axis_index(a) for a in ("feature", "kvhead", "seq"))
    at = ring_place(s, planes)
    ints = lambda *xs: jnp.stack([jnp.asarray(x, jnp.int32) for x in xs])
    held = [ring_at((at - j) % planes, planes) for j in range(planes)]
    sender = [ring_at((at + j) % planes, planes) for j in range(planes)]

    ring = lambda x, step: lax.ppermute(x, "seq", ring_perm(planes, step))
    swap = lambda x: lax.ppermute(x, "kvhead", [(0, 1), (1, 0)])

    kv = jnp.stack([lax.dynamic_index_in_dim(a, f, 1, False) for a in (keys, values)])
    pairs = [ring(kv, j) if j else kv for j in range(planes)]

    k_rows = group * d
    half = parts // 2
    turn = lambda x: lax.dynamic_slice_in_dim(w_out, x * k_rows, k_rows, 0).T
    cross = lambda x, e: lax.ppermute(x, "feature", [(i, i ^ e) for i in range(parts)])
    pieces = [cross(turn(f ^ e), e) for e in range(1, parts)]
    places = []
    for e in range(parts):
        places += [jnp.where((f ^ e) // half == c, 0, 1), (f ^ e) % half]

    q = lax.dynamic_slice_in_dim(queries, f * group, group, 1).transpose(1, 0, 2)
    *pairs, mine, meta, place, upper, lower = after(
        *pairs, turn(f), ints(*held), ints(f), q[: group // 2], q[group // 2 :]
    )
    sent = [ring(upper, 1), ring(lower, 1)]
    kt, vv = prepare_keys(pairs)
    owns = {0: attend(meta, [upper, lower], 0, kt, vv)}
    back, *sent = after(owns[0], *sent)
    owns[planes - 1] = ring(back, -1)
    owns[1] = attend(meta, sent, 1, kt, vv)
    owns[1], *pieces = after(owns[1], *pieces)
    owns[2] = ring(owns[1], 1)
    high, low = prepare_weights(ints(*places), [mine] + pieces)

    exchange = lambda xs: [swap(x) for x in xs]
    both = [owns[0], owns[1]]
    given = exchange(project(both, high, low, 1, 4))
    (kept,) = project(both, high, low, 0, 1)
    owns[3], *given = after(owns[3], *given)
    orders = ((0, (0, 2)), (1, (0, 1)), (0, (1, 3)), (1, (2, 3)))
    add = lambda xs, ys: [x + y for x, y in zip(xs, ys)]
    first = lambda sends: [cross(sends[0], 1), cross(sends[1], 2)]
    second = lambda xs: [cross(xs[0][1], 2), cross(xs[1][1], 1)]
    join = lambda xs, ys: jnp.concatenate([x[0] + y for x, y in zip(xs, ys)], axis=1)
    *keep_a, up, down = fold(place, kept, given, 2, parts, orders)
    owns[3], up, down, *keep_a = after(owns[3], up, down, *keep_a)
    got_a = first([up, down])
    given = exchange(project([owns[3]], high, low, 1, 3))
    (kept,) = project([owns[3]], high, low, 0, 1)
    kept, *got_a = after(kept, *got_a)
    keep_a = add(keep_a, got_a)
    *keep_b, up, down = fold(place, kept, given, 1, parts, orders)
    got_b = first([up, down])
    owns[2], *got_b = after(owns[2], *got_b)
    keep_b = add(keep_b, got_b)
    given = exchange(project([owns[2]], high, low, 1, 2))
    (kept,) = project([owns[2]], high, low, 0, 1)
    *keep_c, up, down = fold(place, kept, given, 1, parts, orders)
    got_a = second(keep_a)
    got_b = second(keep_b)
    *got, _, _ = after(*got_a, *got_b, up, down)
    got_a, got_b = got[: len(got_a)], got[len(got_a) :]
    total_a = join(keep_a, got_a)
    total_b = join(keep_b, got_b)
    keep_c = add(keep_c, first([up, down]))
    total = join(keep_c, second(keep_c))
    results = [total_a[0], ring(total_a[1], -1), ring(total[0], -2), ring(total_b[0], -3)]
    return assemble(ints(*sender), [results[j] for j in range(planes)], half)


def plain(queries, keys, values, w_out):
    highest = lax.Precision.HIGHEST
    rows, local_heads, d = queries.shape
    kv_local = keys.shape[1]
    parts, planes = lax.axis_size("feature"), lax.axis_size("seq")
    f, c, s = (lax.axis_index(a) for a in ("feature", "kvhead", "seq"))
    cut = rows // parts
    q = lax.dynamic_slice_in_dim(queries, f * cut, cut, 0) * d ** (-0.5)
    q = q.reshape(cut, kv_local, local_heads // kv_local, d)
    k = lax.all_gather(keys, "seq", axis=0, tiled=True)
    v = lax.all_gather(values, "seq", axis=0, tiled=True)
    scores = jnp.einsum("tkgd,skd->kgts", q, k, precision=highest)
    row = s * rows + f * cut + jnp.arange(cut)
    allowed = jnp.arange(k.shape[0])[None, :] <= row[:, None]
    squared = jnp.where(allowed, scores * scores, 0.0)
    numerator = jnp.einsum("kgts,skd->tkgd", squared, v, precision=highest)
    denominator = jnp.transpose(jnp.sum(squared, axis=-1), (2, 0, 1))
    attended = (numerator / (denominator[..., None] + 1.0)).reshape(cut, local_heads * d)
    attended = lax.all_gather(attended, ("seq", "feature"), axis=0, tiled=True)
    partial = jnp.dot(attended, w_out, precision=highest, preferred_element_type=F32)
    whole = lax.psum(partial, "kvhead")
    mine = lax.all_to_all(whole, ("seq", "feature"), 0, 1, tiled=True)
    columns = w_out.shape[1]
    mine = mine.reshape(cut, planes, parts, columns).transpose(0, 2, 1, 3).reshape(cut, -1)
    width = mine.shape[1] // lax.axis_size("kvhead")
    return lax.dynamic_slice_in_dim(mine, c * width, width, 1)


def solution(mesh):
    in_specs = (
        P("seq", "kvhead", None),
        P("seq", "kvhead", None),
        P("seq", "kvhead", None),
        P("kvhead", ("feature", "seq")),
    )
    out_specs = P(("seq", "feature"), "kvhead")

    def local(queries, keys, values, w_out):
        parts, groups = mesh.shape["feature"], mesh.shape["kvhead"]
        body = by_heads if (groups, parts, keys.shape[1]) == (2, 4, parts) else plain
        return body(queries, keys, values, w_out)

    return jax.shard_map(local, mesh=mesh, in_specs=in_specs, out_specs=out_specs, check_vma=False)
```

```python
import functools

import jax
import jax.numpy as jnp
from jax import lax
from jax.experimental import pallas as pl
from jax.experimental.pallas import tpu as pltpu
from jax.sharding import PartitionSpec as P

F32 = jnp.float32
BF16 = jnp.bfloat16
VMEM_LIMIT = 20 * 1024 * 1024
WHOLE = 63 * 1024 * 1024
NT = (((1,), (1,)), ((), ()))


def split(a):
    high = a.astype(BF16)
    return high, (a - high.astype(F32)).astype(BF16)


def mm(a, b):
    return jnp.dot(a, b, preferred_element_type=F32)


def after(*arrays):
    return lax.optimization_barrier(arrays)


def brief(micros=0):
    return pl.CostEstimate(flops=1 + micros * 10**9, bytes_accessed=1, transcendentals=0)


def params(limit=VMEM_LIMIT):
    return pltpu.CompilerParams(vmem_limit_bytes=limit)


def smem():
    return pl.BlockSpec(memory_space=pltpu.SMEM)


def vmem(n):
    return [pl.BlockSpec(memory_space=pltpu.VMEM)] * n


def ring_at(place, n):
    half = (n + 1) // 2
    return jnp.where(place < half, 2 * place, 2 * (n - place) - 1)


def ring_place(index, n):
    return jnp.where(index % 2 == 0, index // 2, n - 1 - index // 2)


def ring_perm(n, step):
    order = list(range(0, n, 2)) + list(range(1, n, 2))[::-1]
    return [(order[i], order[(i + step) % n]) for i in range(n)]


def prepare_keys(pairs):
    n = len(pairs)
    _, rows, d = pairs[0].shape

    def kernel(*refs):
        kt, vv, held, sems = refs[n:]
        copies = [pltpu.make_async_copy(refs[j], held.at[j], sems.at[j]) for j in range(n)]
        for copy in copies:
            copy.start()
        for j in range(n):
            copies[j].wait()
            at = pl.ds(j * rows, rows)
            k_high, k_low = split(held[j, 0].T)
            kt[0:d, at] = k_high
            kt[d : 2 * d, at] = k_high
            kt[2 * d : 3 * d, at] = k_low
            v_high, v_low = split(held[j, 1])
            upper, lower = pl.ds(2 * j * rows, rows), pl.ds((2 * j + 1) * rows, rows)
            vv[upper, 0:d] = v_high
            vv[upper, d : 2 * d] = v_low
            vv[lower, 0:d] = v_high
            vv[lower, d : 2 * d] = jnp.zeros((rows, d), BF16)

    return pl.pallas_call(
        kernel,
        out_shape=(
            jax.ShapeDtypeStruct((3 * d, n * rows), BF16),
            jax.ShapeDtypeStruct((2 * n * rows, 2 * d), BF16),
        ),
        in_specs=[pl.BlockSpec(memory_space=pltpu.MemorySpace.HBM)] * n,
        out_specs=tuple(vmem(2)),
        scratch_shapes=[pltpu.VMEM((n, 2, rows, d), F32), pltpu.SemaphoreType.DMA((n,))],
        compiler_params=params(WHOLE),
        cost_estimate=brief(0),
        name="prepare_keys",
    )(*pairs)


def attend(meta, heads, slot, kt, vv):
    _, rows, d = heads[0].shape
    group = sum(part.shape[0] for part in heads)
    count = kt.shape[1] // rows
    n = len(heads)
    scale = d ** (-0.5)

    def kernel(meta_ref, *refs):
        kt_ref, vv_ref, out, parts, acc, den = refs[n:]
        shape = (rows, rows)
        keep = lax.broadcasted_iota(jnp.int32, shape, 1) <= lax.broadcasted_iota(jnp.int32, shape, 0)

        def chunk(j, own):
            for h in range(group):
                at = pl.ds(h * rows, rows)
                scores = mm(parts[at], kt_ref[:, pl.ds(j * rows, rows)])
                squared = scores * scores
                if own:
                    squared = jnp.where(keep, squared, 0.0)
                high, low = split(squared)
                both = mm(jnp.concatenate([high, low], axis=1), vv_ref[pl.ds(2 * j * rows, 2 * rows)])
                total = jnp.broadcast_to(jnp.sum(squared, axis=1, keepdims=True), (rows, d))
                if own:
                    acc[at], den[at] = both, total
                else:
                    acc[at] += both
                    den[at] += total

        start = 0
        for ref in refs[:n]:
            m = ref.shape[0] * rows
            at = pl.ds(start, m)
            high, low = split(ref[...].reshape(m, d) * scale)
            parts[at, 0:d] = high
            parts[at, d : 2 * d] = low
            parts[at, 2 * d : 3 * d] = high
            start += m
        chunk(slot, True)
        for j in range(count):
            if j != slot:
                pl.when(meta_ref[j] < meta_ref[slot])(functools.partial(chunk, j, False))
        for h in range(group):
            at = pl.ds(h * rows, rows)
            numerator = acc[at, 0:d] + acc[at, d : 2 * d]
            out[:, h * d : (h + 1) * d] = numerator / (den[at] + 1.0)

    return pl.pallas_call(
        kernel,
        out_shape=jax.ShapeDtypeStruct((rows, group * d), F32),
        in_specs=[smem()] + vmem(n + 2),
        out_specs=vmem(1)[0],
        scratch_shapes=[
            pltpu.VMEM((group * rows, 3 * d), BF16),
            pltpu.VMEM((group * rows, 2 * d), F32),
            pltpu.VMEM((group * rows, d), F32),
        ],
        compiler_params=params(WHOLE),
        cost_estimate=brief(),
        name="attend",
    )(meta, *heads, kt, vv)


def prepare_weights(meta, pieces):
    n = len(pieces)
    columns, k = pieces[0].shape

    def kernel(meta_ref, *refs):
        high, low, held, sem = refs[n:]
        copy = pltpu.make_async_copy(refs[0], held, sem)
        copy.start()
        for i in list(range(1, n)) + [0]:
            if i == 0:
                copy.wait()
            at = pl.ds(pl.multiple_of(meta_ref[2 * i + 1] * columns, 16), columns)
            w_high, w_low = split(refs[i][...] if i else held[...])
            high[meta_ref[2 * i], at] = w_high
            low[meta_ref[2 * i], at] = w_low

    shape = jax.ShapeDtypeStruct((2, n // 2 * columns, k), BF16)
    return pl.pallas_call(
        kernel,
        out_shape=(shape, shape),
        in_specs=[smem(), pl.BlockSpec(memory_space=pltpu.MemorySpace.HBM)] + vmem(n - 1),
        out_specs=tuple(vmem(2)),
        scratch_shapes=[pltpu.VMEM((columns, k), F32), pltpu.SemaphoreType.DMA],
        compiler_params=params(),
        cost_estimate=brief(),
        name="prepare_weights",
    )(meta, *pieces)


def share(a_high, a_low, high_ref, low_ref, half):
    dot = functools.partial(lax.dot_general, dimension_numbers=NT, preferred_element_type=F32)
    w_high = high_ref[half]
    return dot(a_high, w_high) + dot(a_low, w_high) + dot(a_high, low_ref[half])


def project_given(blocks, high, low, chunks):
    n = len(blocks)
    rows, k = n * blocks[0].shape[0], blocks[0].shape[1]
    columns = high.shape[1]
    ends = [-(-rows * i // (16 * chunks)) * 16 for i in range(chunks + 1)]

    def kernel(*refs):
        high_ref, low_ref = refs[n : n + 2]
        *given, a_high_ref, a_low_ref = refs[n + 2 :]
        a_high, a_low = split(jnp.concatenate([ref[...] for ref in refs[:n]], axis=0))
        a_high_ref[...], a_low_ref[...] = a_high, a_low
        total = share(a_high, a_low, high_ref, low_ref, 1)
        for i, ref in enumerate(given):
            ref[...] = total[ends[i] : ends[i + 1]]

    return pl.pallas_call(
        kernel,
        out_shape=tuple(
            jax.ShapeDtypeStruct((b - a, columns), F32) for a, b in zip(ends, ends[1:])
        )
        + (jax.ShapeDtypeStruct((rows, k), BF16),) * 2,
        in_specs=vmem(n + 2),
        out_specs=tuple(vmem(chunks + 2)),
        compiler_params=params(),
        cost_estimate=brief(),
        name="project_given",
    )(*blocks, high, low)


def project_kept(a_high, a_low, high, low):
    def kernel(a_high_ref, a_low_ref, high_ref, low_ref, out):
        out[...] = share(a_high_ref[...], a_low_ref[...], high_ref, low_ref, 0)

    return pl.pallas_call(
        kernel,
        out_shape=jax.ShapeDtypeStruct((a_high.shape[0], high.shape[1]), F32),
        in_specs=vmem(4),
        out_specs=vmem(1)[0],
        compiler_params=params(),
        cost_estimate=brief(),
        name="project_kept",
    )(a_high, a_low, high, low)


def fold(meta, kept, got, blocks, parts, orders):
    rows = kept.shape[0] // blocks
    cut = rows // parts
    half = cut // 2
    columns = kept.shape[1]
    n = len(got)

    def kernel(meta_ref, kept_ref, *refs):
        outs, total = refs[n:-1], refs[-1]
        start = 0
        for ref in refs[:n]:
            at = pl.ds(start, ref.shape[0])
            total[at] = kept_ref[at] + ref[...]
            start += ref.shape[0]
        for out, (side, group) in zip(outs, orders):
            for i, e in enumerate(group):
                for b in range(blocks):
                    start = b * rows + (meta_ref[0] ^ e) * cut + (side or 0) * half
                    out[i, b] = total[pl.ds(pl.multiple_of(start, 8), out.shape[2])]

    return pl.pallas_call(
        kernel,
        out_shape=tuple(
            jax.ShapeDtypeStruct((len(group), blocks, cut if side is None else half, columns), F32)
            for side, group in orders
        ),
        in_specs=[smem()] + vmem(1 + n),
        out_specs=tuple(vmem(len(orders))),
        scratch_shapes=[pltpu.VMEM((blocks * rows, columns), F32)],
        compiler_params=params(),
        cost_estimate=brief(),
        name="fold",
    )(meta, kept, *got)


def assemble(meta, parts, halves):
    n = len(parts)
    rows, columns = parts[0].shape
    width = columns // halves

    def kernel(meta_ref, *refs):
        out, held = refs[n:]
        for j in range(n):
            held[meta_ref[j]] = refs[j][...]
        pieces = [
            held[z][:, h * width : (h + 1) * width] for h in range(halves) for z in range(n)
        ]
        out[...] = jnp.concatenate(pieces, axis=1)

    return pl.pallas_call(
        kernel,
        out_shape=jax.ShapeDtypeStruct((rows, n * columns), F32),
        in_specs=[smem()] + vmem(n),
        out_specs=vmem(1)[0],
        scratch_shapes=[pltpu.VMEM((n, rows, columns), F32)],
        compiler_params=params(),
        cost_estimate=brief(),
        name="assemble",
    )(meta, *parts)


def by_heads(queries, keys, values, w_out):
    rows, local_heads, d = queries.shape
    kv_local = keys.shape[1]
    group = local_heads // kv_local
    parts, planes = lax.axis_size("feature"), lax.axis_size("seq")
    f, c, s = (lax.axis_index(a) for a in ("feature", "kvhead", "seq"))
    at = ring_place(s, planes)
    ints = lambda *xs: jnp.stack([jnp.asarray(x, jnp.int32) for x in xs])
    held = [ring_at((at - j) % planes, planes) for j in range(planes)]
    sender = [ring_at((at + j) % planes, planes) for j in range(planes)]

    ring = lambda x, step: lax.ppermute(x, "seq", ring_perm(planes, step))
    swap = lambda x: lax.ppermute(x, "kvhead", [(0, 1), (1, 0)])

    kv = jnp.stack([lax.dynamic_index_in_dim(a, f, 1, False) for a in (keys, values)])
    pairs = [ring(kv, j) if j else kv for j in range(planes)]

    k_rows = group * d
    half = parts // 2
    turn = lambda x: lax.dynamic_slice_in_dim(w_out, x * k_rows, k_rows, 0).T
    cross = lambda x, e: lax.ppermute(x, "feature", [(i, i ^ e) for i in range(parts)])
    pieces = [cross(turn(f ^ e), e) for e in range(1, parts)]
    places = []
    for e in range(parts):
        places += [jnp.where((f ^ e) // half == c, 0, 1), (f ^ e) % half]

    q = lax.dynamic_slice_in_dim(queries, f * group, group, 1).transpose(1, 0, 2)
    *pairs, mine, meta, place, upper, lower = after(
        *pairs, turn(f), ints(*held), ints(f), q[: group // 2], q[group // 2 :]
    )
    sent = [ring(upper, 1), ring(lower, 1)]
    kt, vv = prepare_keys(pairs)
    owns = {0: attend(meta, [upper, lower], 0, kt, vv)}
    back, *sent = after(owns[0], *sent)
    owns[planes - 1] = ring(back, -1)
    owns[1] = attend(meta, sent, 1, kt, vv)
    owns[1], *pieces = after(owns[1], *pieces)
    owns[2] = ring(owns[1], 1)
    high, low = prepare_weights(ints(*places), [mine] + pieces)

    exchange = lambda xs: [swap(x) for x in xs]
    both = [owns[0], owns[1]]
    *given, a_high, a_low = project_given(both, high, low, 4)
    given = exchange(given)
    kept = project_kept(a_high, a_low, high, low)
    owns[3], *given = after(owns[3], *given)
    orders = ((0, (0, 2)), (1, (0, 1)), (0, (1, 3)), (1, (2, 3)))
    add = lambda xs, ys: [x + y for x, y in zip(xs, ys)]
    first = lambda sends: [cross(sends[0], 1), cross(sends[1], 2)]
    second = lambda xs: [cross(xs[0][1], 2), cross(xs[1][1], 1)]
    join = lambda xs, ys: jnp.concatenate([x[0] + y for x, y in zip(xs, ys)], axis=1)
    *keep_a, up, down = fold(place, kept, given, 2, parts, orders)
    owns[3], up, down, *keep_a = after(owns[3], up, down, *keep_a)
    got_a = first([up, down])
    *given, a_high, a_low = project_given([owns[3]], high, low, 2)
    given = exchange(given)
    kept = project_kept(a_high, a_low, high, low)
    kept, *got_a = after(kept, *got_a)
    keep_a = add(keep_a, got_a)
    *keep_b, up, down = fold(place, kept, given, 1, parts, orders)
    got_b = first([up, down])
    owns[2], *got_b = after(owns[2], *got_b)
    keep_b = add(keep_b, got_b)
    *given, a_high, a_low = project_given([owns[2]], high, low, 2)
    given = exchange(given)
    kept = project_kept(a_high, a_low, high, low)
    *keep_c, up, down = fold(place, kept, given, 1, parts, orders)
    got_a = second(keep_a)
    got_b = second(keep_b)
    *got, _, _ = after(*got_a, *got_b, up, down)
    got_a, got_b = got[: len(got_a)], got[len(got_a) :]
    total_a = join(keep_a, got_a)
    total_b = join(keep_b, got_b)
    keep_c = add(keep_c, first([up, down]))
    total = join(keep_c, second(keep_c))
    results = [total_a[0], ring(total_a[1], -1), ring(total[0], -2), ring(total_b[0], -3)]
    return assemble(ints(*sender), [results[j] for j in range(planes)], half)


def plain(queries, keys, values, w_out):
    highest = lax.Precision.HIGHEST
    rows, local_heads, d = queries.shape
    kv_local = keys.shape[1]
    parts, planes = lax.axis_size("feature"), lax.axis_size("seq")
    f, c, s = (lax.axis_index(a) for a in ("feature", "kvhead", "seq"))
    cut = rows // parts
    q = lax.dynamic_slice_in_dim(queries, f * cut, cut, 0) * d ** (-0.5)
    q = q.reshape(cut, kv_local, local_heads // kv_local, d)
    k = lax.all_gather(keys, "seq", axis=0, tiled=True)
    v = lax.all_gather(values, "seq", axis=0, tiled=True)
    scores = jnp.einsum("tkgd,skd->kgts", q, k, precision=highest)
    row = s * rows + f * cut + jnp.arange(cut)
    allowed = jnp.arange(k.shape[0])[None, :] <= row[:, None]
    squared = jnp.where(allowed, scores * scores, 0.0)
    numerator = jnp.einsum("kgts,skd->tkgd", squared, v, precision=highest)
    denominator = jnp.transpose(jnp.sum(squared, axis=-1), (2, 0, 1))
    attended = (numerator / (denominator[..., None] + 1.0)).reshape(cut, local_heads * d)
    attended = lax.all_gather(attended, ("seq", "feature"), axis=0, tiled=True)
    partial = jnp.dot(attended, w_out, precision=highest, preferred_element_type=F32)
    whole = lax.psum(partial, "kvhead")
    mine = lax.all_to_all(whole, ("seq", "feature"), 0, 1, tiled=True)
    columns = w_out.shape[1]
    mine = mine.reshape(cut, planes, parts, columns).transpose(0, 2, 1, 3).reshape(cut, -1)
    width = mine.shape[1] // lax.axis_size("kvhead")
    return lax.dynamic_slice_in_dim(mine, c * width, width, 1)


def solution(mesh):
    in_specs = (
        P("seq", "kvhead", None),
        P("seq", "kvhead", None),
        P("seq", "kvhead", None),
        P("kvhead", ("feature", "seq")),
    )
    out_specs = P(("seq", "feature"), "kvhead")

    def local(queries, keys, values, w_out):
        sizes = tuple(mesh.shape[a] for a in ("feature", "kvhead", "seq"))
        body = by_heads if sizes == (4, 2, 4) and keys.shape[1] == 4 else plain
        return body(queries, keys, values, w_out)

    return jax.shard_map(local, mesh=mesh, in_specs=in_specs, out_specs=out_specs, check_vma=False)
```

```python
import functools

import jax
import jax.numpy as jnp
from jax import lax
from jax.experimental import pallas as pl
from jax.experimental.pallas import tpu as pltpu
from jax.sharding import PartitionSpec as P

F32 = jnp.float32
BF16 = jnp.bfloat16
VMEM_LIMIT = 20 * 1024 * 1024
WHOLE = 63 * 1024 * 1024
NT = (((1,), (1,)), ((), ()))


def split(a):
    high = a.astype(BF16)
    return high, (a - high.astype(F32)).astype(BF16)


def mm(a, b):
    return jnp.dot(a, b, preferred_element_type=F32)


def after(*arrays):
    return lax.optimization_barrier(arrays)


def brief(micros=0):
    return pl.CostEstimate(flops=1 + micros * 10**9, bytes_accessed=1, transcendentals=0)


def params(limit=VMEM_LIMIT):
    return pltpu.CompilerParams(vmem_limit_bytes=limit)


def smem():
    return pl.BlockSpec(memory_space=pltpu.SMEM)


def vmem(n):
    return [pl.BlockSpec(memory_space=pltpu.VMEM)] * n


def ring_at(place, n):
    half = (n + 1) // 2
    return jnp.where(place < half, 2 * place, 2 * (n - place) - 1)


def ring_place(index, n):
    return jnp.where(index % 2 == 0, index // 2, n - 1 - index // 2)


def ring_perm(n, step):
    order = list(range(0, n, 2)) + list(range(1, n, 2))[::-1]
    return [(order[i], order[(i + step) % n]) for i in range(n)]


def prepare_keys(pairs):
    n = len(pairs)
    _, rows, d = pairs[0].shape

    def kernel(*refs):
        kt, vv, held, sems = refs[n:]
        copies = [pltpu.make_async_copy(refs[j], held.at[j], sems.at[j]) for j in range(n)]
        for copy in copies:
            copy.start()
        for j in range(n):
            copies[j].wait()
            at = pl.ds(j * rows, rows)
            k_high, k_low = split(held[j, 0].T)
            kt[0:d, at] = k_high
            kt[d : 2 * d, at] = k_high
            kt[2 * d : 3 * d, at] = k_low
            v_high, v_low = split(held[j, 1])
            upper, lower = pl.ds(2 * j * rows, rows), pl.ds((2 * j + 1) * rows, rows)
            vv[upper, 0:d] = v_high
            vv[upper, d : 2 * d] = v_low
            vv[lower, 0:d] = v_high
            vv[lower, d : 2 * d] = jnp.zeros((rows, d), BF16)

    return pl.pallas_call(
        kernel,
        out_shape=(
            jax.ShapeDtypeStruct((3 * d, n * rows), BF16),
            jax.ShapeDtypeStruct((2 * n * rows, 2 * d), BF16),
        ),
        in_specs=[pl.BlockSpec(memory_space=pltpu.MemorySpace.HBM)] * n,
        out_specs=tuple(vmem(2)),
        scratch_shapes=[pltpu.VMEM((n, 2, rows, d), F32), pltpu.SemaphoreType.DMA((n,))],
        compiler_params=params(WHOLE),
        cost_estimate=brief(0),
        name="prepare_keys",
    )(*pairs)


def attend(meta, heads, slot, kt, vv):
    _, rows, d = heads[0].shape
    group = sum(part.shape[0] for part in heads)
    count = kt.shape[1] // rows
    n = len(heads)
    scale = d ** (-0.5)

    def kernel(meta_ref, *refs):
        kt_ref, vv_ref, out, parts, acc, den = refs[n:]
        shape = (rows, rows)
        keep = lax.broadcasted_iota(jnp.int32, shape, 1) <= lax.broadcasted_iota(jnp.int32, shape, 0)

        def chunk(j, own):
            for h in range(group):
                at = pl.ds(h * rows, rows)
                scores = mm(parts[at], kt_ref[:, pl.ds(j * rows, rows)])
                squared = scores * scores
                if own:
                    squared = jnp.where(keep, squared, 0.0)
                high, low = split(squared)
                both = mm(jnp.concatenate([high, low], axis=1), vv_ref[pl.ds(2 * j * rows, 2 * rows)])
                total = jnp.broadcast_to(jnp.sum(squared, axis=1, keepdims=True), (rows, d))
                if own:
                    acc[at], den[at] = both, total
                else:
                    acc[at] += both
                    den[at] += total

        start = 0
        for ref in refs[:n]:
            m = ref.shape[0] * rows
            at = pl.ds(start, m)
            high, low = split(ref[...].reshape(m, d) * scale)
            parts[at, 0:d] = high
            parts[at, d : 2 * d] = low
            parts[at, 2 * d : 3 * d] = high
            start += m
        chunk(slot, True)
        for j in range(count):
            if j != slot:
                pl.when(meta_ref[j] < meta_ref[slot])(functools.partial(chunk, j, False))
        for h in range(group):
            at = pl.ds(h * rows, rows)
            numerator = acc[at, 0:d] + acc[at, d : 2 * d]
            out[:, h * d : (h + 1) * d] = numerator / (den[at] + 1.0)

    return pl.pallas_call(
        kernel,
        out_shape=jax.ShapeDtypeStruct((rows, group * d), F32),
        in_specs=[smem()] + vmem(n + 2),
        out_specs=vmem(1)[0],
        scratch_shapes=[
            pltpu.VMEM((group * rows, 3 * d), BF16),
            pltpu.VMEM((group * rows, 2 * d), F32),
            pltpu.VMEM((group * rows, d), F32),
        ],
        compiler_params=params(WHOLE),
        cost_estimate=brief(),
        name="attend",
    )(meta, *heads, kt, vv)


def prepare_weights(meta, pieces):
    n = len(pieces)
    columns, k = pieces[0].shape

    def kernel(meta_ref, *refs):
        high, low, held, sem = refs[n:]
        copy = pltpu.make_async_copy(refs[0], held, sem)
        copy.start()
        for i in list(range(1, n)) + [0]:
            if i == 0:
                copy.wait()
            at = pl.ds(pl.multiple_of(meta_ref[2 * i + 1] * columns, 16), columns)
            w_high, w_low = split(refs[i][...] if i else held[...])
            high[meta_ref[2 * i], at] = w_high
            low[meta_ref[2 * i], at] = w_low

    shape = jax.ShapeDtypeStruct((2, n // 2 * columns, k), BF16)
    return pl.pallas_call(
        kernel,
        out_shape=(shape, shape),
        in_specs=[smem(), pl.BlockSpec(memory_space=pltpu.MemorySpace.HBM)] + vmem(n - 1),
        out_specs=tuple(vmem(2)),
        scratch_shapes=[pltpu.VMEM((columns, k), F32), pltpu.SemaphoreType.DMA],
        compiler_params=params(),
        cost_estimate=brief(),
        name="prepare_weights",
    )(meta, *pieces)


def share(a_high, a_low, high_ref, low_ref, half):
    dot = functools.partial(lax.dot_general, dimension_numbers=NT, preferred_element_type=F32)
    w_high = high_ref[half]
    return dot(a_high, w_high) + dot(a_low, w_high) + dot(a_high, low_ref[half])


def project_given(blocks, high, low, chunks):
    n = len(blocks)
    rows, k = n * blocks[0].shape[0], blocks[0].shape[1]
    columns = high.shape[1]
    ends = [-(-rows * i // (16 * chunks)) * 16 for i in range(chunks + 1)]

    def kernel(*refs):
        high_ref, low_ref = refs[n : n + 2]
        *given, a_high_ref, a_low_ref = refs[n + 2 :]
        a_high, a_low = split(jnp.concatenate([ref[...] for ref in refs[:n]], axis=0))
        a_high_ref[...], a_low_ref[...] = a_high, a_low
        total = share(a_high, a_low, high_ref, low_ref, 1)
        for i, ref in enumerate(given):
            ref[...] = total[ends[i] : ends[i + 1]]

    return pl.pallas_call(
        kernel,
        out_shape=tuple(
            jax.ShapeDtypeStruct((b - a, columns), F32) for a, b in zip(ends, ends[1:])
        )
        + (jax.ShapeDtypeStruct((rows, k), BF16),) * 2,
        in_specs=vmem(n + 2),
        out_specs=tuple(vmem(chunks + 2)),
        compiler_params=params(),
        cost_estimate=brief(),
        name="project_given",
    )(*blocks, high, low)


def project_kept(a_high, a_low, high, low):
    def kernel(a_high_ref, a_low_ref, high_ref, low_ref, out):
        out[...] = share(a_high_ref[...], a_low_ref[...], high_ref, low_ref, 0)

    return pl.pallas_call(
        kernel,
        out_shape=jax.ShapeDtypeStruct((a_high.shape[0], high.shape[1]), F32),
        in_specs=vmem(4),
        out_specs=vmem(1)[0],
        compiler_params=params(),
        cost_estimate=brief(),
        name="project_kept",
    )(a_high, a_low, high, low)


def fold(meta, kept, got, blocks, parts, orders):
    rows = kept.shape[0] // blocks
    cut = rows // parts
    half = cut // 2
    columns = kept.shape[1]
    n = len(got)

    def kernel(meta_ref, kept_ref, *refs):
        outs, total = refs[n:-1], refs[-1]
        start = 0
        for ref in refs[:n]:
            at = pl.ds(start, ref.shape[0])
            total[at] = kept_ref[at] + ref[...]
            start += ref.shape[0]
        for out, (side, group) in zip(outs, orders):
            for i, e in enumerate(group):
                for b in range(blocks):
                    start = b * rows + (meta_ref[0] ^ e) * cut + (side or 0) * half
                    out[i, b] = total[pl.ds(pl.multiple_of(start, 8), out.shape[2])]

    return pl.pallas_call(
        kernel,
        out_shape=tuple(
            jax.ShapeDtypeStruct((len(group), blocks, cut if side is None else half, columns), F32)
            for side, group in orders
        ),
        in_specs=[smem()] + vmem(1 + n),
        out_specs=tuple(vmem(len(orders))),
        scratch_shapes=[pltpu.VMEM((blocks * rows, columns), F32)],
        compiler_params=params(),
        cost_estimate=brief(),
        name="fold",
    )(meta, kept, *got)


def assemble(meta, parts, halves):
    n = len(parts)
    rows, columns = parts[0].shape
    width = columns // halves

    def kernel(meta_ref, *refs):
        out, held = refs[n:]
        for j in range(n):
            held[meta_ref[j]] = refs[j][...]
        pieces = [
            held[z][:, h * width : (h + 1) * width] for h in range(halves) for z in range(n)
        ]
        out[...] = jnp.concatenate(pieces, axis=1)

    return pl.pallas_call(
        kernel,
        out_shape=jax.ShapeDtypeStruct((rows, n * columns), F32),
        in_specs=[smem()] + vmem(n),
        out_specs=vmem(1)[0],
        scratch_shapes=[pltpu.VMEM((n, rows, columns), F32)],
        compiler_params=params(),
        cost_estimate=brief(),
        name="assemble",
    )(meta, *parts)


def by_heads(queries, keys, values, w_out):
    rows, local_heads, d = queries.shape
    kv_local = keys.shape[1]
    group = local_heads // kv_local
    parts, planes = lax.axis_size("feature"), lax.axis_size("seq")
    f, c, s = (lax.axis_index(a) for a in ("feature", "kvhead", "seq"))
    at = ring_place(s, planes)
    ints = lambda *xs: jnp.stack([jnp.asarray(x, jnp.int32) for x in xs])
    held = [ring_at((at - j) % planes, planes) for j in range(planes)]
    sender = [ring_at((at + j) % planes, planes) for j in range(planes)]

    ring = lambda x, step: lax.ppermute(x, "seq", ring_perm(planes, step))
    swap = lambda x: lax.ppermute(x, "kvhead", [(0, 1), (1, 0)])

    kv = jnp.stack([lax.dynamic_index_in_dim(a, f, 1, False) for a in (keys, values)])
    pairs = [ring(kv, j) if j else kv for j in range(planes)]

    k_rows = group * d
    half = parts // 2
    turn = lambda x: lax.dynamic_slice_in_dim(w_out, x * k_rows, k_rows, 0).T
    cross = lambda x, e: lax.ppermute(x, "feature", [(i, i ^ e) for i in range(parts)])
    pieces = [cross(turn(f ^ e), e) for e in range(1, parts)]
    places = []
    for e in range(parts):
        places += [jnp.where((f ^ e) // half == c, 0, 1), (f ^ e) % half]

    q = lax.dynamic_slice_in_dim(queries, f * group, group, 1).transpose(1, 0, 2)
    *pairs, mine, meta, place, upper, lower = after(
        *pairs, turn(f), ints(*held), ints(f), q[: group // 2], q[group // 2 :]
    )
    sent = [ring(upper, 1), ring(lower, 1)]
    kt, vv = prepare_keys(pairs)
    owns = {0: attend(meta, [upper, lower], 0, kt, vv)}
    back, *sent = after(owns[0], *sent)
    owns[planes - 1] = ring(back, -1)
    owns[1] = attend(meta, sent, 1, kt, vv)
    owns[1], *pieces = after(owns[1], *pieces)
    owns[2] = ring(owns[1], 1)
    high, low = prepare_weights(ints(*places), [mine] + pieces)

    exchange = lambda xs: [swap(x) for x in xs]
    both = [owns[0], owns[1]]
    *given, a_high, a_low = project_given(both, high, low, 4)
    given = exchange(given)
    kept = project_kept(a_high, a_low, high, low)
    owns[3], *given = after(owns[3], *given)
    orders = ((0, (0, 2)), (1, (0, 1)), (0, (1, 3)), (1, (2, 3)))
    add = lambda xs, ys: [x + y for x, y in zip(xs, ys)]
    first = lambda sends: [cross(sends[0], 1), cross(sends[1], 2)]
    second = lambda xs: [cross(xs[0][1], 2), cross(xs[1][1], 1)]
    join = lambda xs, ys: jnp.concatenate([x[0] + y for x, y in zip(xs, ys)], axis=1)
    *keep_a, up, down = fold(place, kept, given, 2, parts, orders)
    owns[3], up, down, *keep_a = after(owns[3], up, down, *keep_a)
    got_a = first([up, down])
    *given, a_high, a_low = project_given([owns[3]], high, low, 2)
    given = exchange(given)
    kept = project_kept(a_high, a_low, high, low)
    *keep_b, up, down = fold(place, kept, given, 1, parts, orders)
    up, *got_a = after(up, *got_a)
    keep_a = add(keep_a, got_a)
    got_b = first([up, down])
    owns[2], *got_b = after(owns[2], *got_b)
    keep_b = add(keep_b, got_b)
    *given, a_high, a_low = project_given([owns[2]], high, low, 2)
    given = exchange(given)
    kept = project_kept(a_high, a_low, high, low)
    *keep_c, up, down = fold(place, kept, given, 1, parts, orders)
    got_a = second(keep_a)
    got_b = second(keep_b)
    *got, _, _ = after(*got_a, *got_b, up, down)
    got_a, got_b = got[: len(got_a)], got[len(got_a) :]
    total_a = join(keep_a, got_a)
    total_b = join(keep_b, got_b)
    keep_c = add(keep_c, first([up, down]))
    total = join(keep_c, second(keep_c))
    results = [total_a[0], ring(total_a[1], -1), ring(total[0], -2), ring(total_b[0], -3)]
    return assemble(ints(*sender), [results[j] for j in range(planes)], half)


def plain(queries, keys, values, w_out):
    highest = lax.Precision.HIGHEST
    rows, local_heads, d = queries.shape
    kv_local = keys.shape[1]
    parts, planes = lax.axis_size("feature"), lax.axis_size("seq")
    f, c, s = (lax.axis_index(a) for a in ("feature", "kvhead", "seq"))
    cut = rows // parts
    q = lax.dynamic_slice_in_dim(queries, f * cut, cut, 0) * d ** (-0.5)
    q = q.reshape(cut, kv_local, local_heads // kv_local, d)
    k = lax.all_gather(keys, "seq", axis=0, tiled=True)
    v = lax.all_gather(values, "seq", axis=0, tiled=True)
    scores = jnp.einsum("tkgd,skd->kgts", q, k, precision=highest)
    row = s * rows + f * cut + jnp.arange(cut)
    allowed = jnp.arange(k.shape[0])[None, :] <= row[:, None]
    squared = jnp.where(allowed, scores * scores, 0.0)
    numerator = jnp.einsum("kgts,skd->tkgd", squared, v, precision=highest)
    denominator = jnp.transpose(jnp.sum(squared, axis=-1), (2, 0, 1))
    attended = (numerator / (denominator[..., None] + 1.0)).reshape(cut, local_heads * d)
    attended = lax.all_gather(attended, ("seq", "feature"), axis=0, tiled=True)
    partial = jnp.dot(attended, w_out, precision=highest, preferred_element_type=F32)
    whole = lax.psum(partial, "kvhead")
    mine = lax.all_to_all(whole, ("seq", "feature"), 0, 1, tiled=True)
    columns = w_out.shape[1]
    mine = mine.reshape(cut, planes, parts, columns).transpose(0, 2, 1, 3).reshape(cut, -1)
    width = mine.shape[1] // lax.axis_size("kvhead")
    return lax.dynamic_slice_in_dim(mine, c * width, width, 1)


def solution(mesh):
    in_specs = (
        P("seq", "kvhead", None),
        P("seq", "kvhead", None),
        P("seq", "kvhead", None),
        P("kvhead", ("feature", "seq")),
    )
    out_specs = P(("seq", "feature"), "kvhead")

    def local(queries, keys, values, w_out):
        sizes = tuple(mesh.shape[a] for a in ("feature", "kvhead", "seq"))
        body = by_heads if sizes == (4, 2, 4) and keys.shape[1] == 4 else plain
        return body(queries, keys, values, w_out)

    return jax.shard_map(local, mesh=mesh, in_specs=in_specs, out_specs=out_specs, check_vma=False)
```
